32 devices in a mesh: dp: 8 (over z, x), row: 2 (over y), col: 2 (over core).
Axes of the slice: x: 2, y: 2, z: 4, core: 2. Of those that a mesh axis runs over, the one named last changes fastest.
Arguments:
- tokens: bfloat16 [6144, 2048], P(('dp', 'row'), 'col'), may hold values from -6 to 6
- seq_lengths: int32 [8, 3], P('dp'), may hold values from 1 to 512, 768 in all within a row
- attn_gain: float32 [2048], P('col'), may hold values from 0.5 to 1.5
- q_weight: bfloat16 [2048, 2048], P('col', 'row'), may hold values from -0.1875 to 0.1875
- k_weight: bfloat16 [2048, 256], P('col', 'row'), may hold values from -0.1875 to 0.1875
- v_weight: bfloat16 [2048, 256], P('col', 'row'), may hold values from -0.125 to 0.125
- o_weight: bfloat16 [2048, 2048], P('row', 'col'), may hold values from -0.5 to 0.5
- ffn_gain: float32 [2048], P('col'), may hold values from 0.5 to 1.5
- gate_weight: bfloat16 [2048, 5632], P('col', 'row'), may hold values from -0.125 to 0.125
- up_weight: bfloat16 [2048, 5632], P('col', 'row'), may hold values from -0.125 to 0.125
- down_weight: bfloat16 [5632, 2048], P('row', 'col'), may hold values from -0.078125 to 0.078125
- out_grad: bfloat16 [6144, 2048], P(('dp', 'row'), 'col'), may hold values from -6 to 6
Outputs:
- result: bfloat16 [6144, 2048], P(('dp', 'row'), 'col')
- grad_tokens: bfloat16 [6144, 2048], P(('dp', 'row'), 'col')
- grad_attn_gain: float32 [2048], P('col')
- grad_q_weight: float32 [2048, 2048], P(('col', 'dp'), 'row')
- grad_k_weight: float32 [2048, 256], P(('col', 'dp'), 'row')
- grad_v_weight: float32 [2048, 256], P(('col', 'dp'), 'row')
- grad_o_weight: float32 [2048, 2048], P(('row', 'dp'), 'col')
- grad_ffn_gain: float32 [2048], P('col')
- grad_gate_weight: float32 [2048, 5632], P(('col', 'dp'), 'row')
- grad_up_weight: float32 [2048, 5632], P(('col', 'dp'), 'row')
- grad_down_weight: float32 [5632, 2048], P(('row', 'dp'), 'col')
The draws below stay inside these ranges and needn't reach their ends.
Inputs may be any that keep to these rules, and one draw needn't show every extreme that they name: `seq_lengths`: each group's 3 lengths sum to 768; the longest of every group has exactly 512 tokens.
All inputs are finite; a program needn't handle non-finite values.
Results may differ from the reference program's by a relative error of at most 0.018.
Values may be sent and summed in bfloat16 or wider, within the bound.
No kernel may reach another device: no remote copies, remote signals or barrier semaphores. Data moves between devices by JAX's collectives and lax.ppermute only.
A program may use at most 192 MiB of HBM per device.

```python
import math
import jax
import jax.numpy as jnp
import numpy as np
from jax import lax

D = 2048
HEADS = 32
KV_HEADS = 4
HEAD_DIM = 64
FF = 5632
TOK_GROUP = 768
NSEQ = 3
LONGEST = 512
TOKENS = 6144
N_DP = 8


def level_of(stream_key, shape, cuts, low, largest):
    gain, own = 1.0, jax.random.fold_in(stream_key, 6)
    for dim, blocks in cuts:
        heights = jnp.exp(jax.random.uniform(jax.random.fold_in(own, dim), (blocks,), jnp.float32, low / len(cuts), largest / len(cuts)))
        gain = gain * jnp.repeat(heights, shape[dim] // blocks).reshape([-1 if axis == dim else 1 for axis in range(len(shape))])
    return gain


def split_up(number_of, total, bound, skew):
    portions = [(1 << 20) // math.isqrt(grade ** skew) + 1 for grade in range(2, number_of + 1)]
    spare, given = total - bound - (number_of - 1), [1] * (number_of - 1)
    while spare > 0:
        free = [i for i in range(number_of - 1) if given[i] < bound]
        whole, budget = sum([portions[i] for i in free]), spare
        for i in free:
            more = min(bound - given[i], max(1, budget * portions[i] // whole), spare)
            given[i] = given[i] + more
            spare = spare - more
    return np.array([bound] + given)


def ragged(key, number_of, total, most, lean):
    if number_of == 2:
        one = jax.random.randint(key, (), max(1, total - most), min(most, total - 1) + 1)
        return jnp.stack([one, total - one])
    sizes = jnp.asarray(split_up(number_of, total, most, lean), jnp.int32)
    pairs = (number_of - 1) // 2
    source_of, receiver = sizes[1:1 + 2 * pairs:2], sizes[2:2 + 2 * pairs:2]
    margin = jnp.minimum(source_of - 1, most - receiver)
    moved = jax.random.randint(jax.random.fold_in(key, 1), (pairs,), 0, 1 << 20) % (margin + 1)
    sizes = sizes.at[1:1 + 2 * pairs:2].set(source_of - moved).at[2:2 + 2 * pairs:2].set(receiver + moved)
    return sizes[jax.random.permutation(jax.random.fold_in(key, 2), number_of)]


def normal_values(own_key, shape, spread, limit, cuts=(), held_as=jnp.bfloat16):
    result = spread * jax.random.normal(own_key, shape, jnp.float32)
    if cuts:
        result = result * level_of(own_key, shape, cuts, -0.22, 0.18)
    return jnp.clip(result, -limit, limit).astype(held_as)


def setup_inputs(seed: int = 0) -> dict:
    splits = jax.random.split(jax.random.key(seed), 13)
    return {
        "tokens": normal_values(splits[0], (TOKENS, D), 1.0, 6.0, ((0, 16), (1, 2))),
        "seq_lengths": jax.vmap(lambda own: ragged(own, NSEQ, TOK_GROUP, LONGEST, 2))(jax.random.split(splits[1], N_DP)).reshape((N_DP, NSEQ)).astype(jnp.int32),
        "attn_gain": jnp.clip(1.0 + 0.1 * jax.random.normal(splits[2], (D,), jnp.float32), 0.5, 1.5),
        "q_weight": normal_values(splits[3], (D, HEADS * HEAD_DIM), (D // 2) ** -0.5, 0.1875, ((0, 2), (1, 2))),
        "k_weight": normal_values(splits[4], (D, KV_HEADS * HEAD_DIM), (D // 2) ** -0.5, 0.1875, ((0, 2), (1, 2))),
        "v_weight": normal_values(splits[5], (D, KV_HEADS * HEAD_DIM), D ** -0.5, 0.125, ((0, 2), (1, 2))),
        "o_weight": normal_values(splits[6], (HEADS * HEAD_DIM, D), (HEADS * HEAD_DIM // 16) ** -0.5, 0.5, ((0, 2), (1, 2))),
        "ffn_gain": jnp.clip(1.0 + 0.1 * jax.random.normal(splits[7], (D,), jnp.float32), 0.5, 1.5),
        "gate_weight": normal_values(splits[8], (D, FF), D ** -0.5, 0.125, ((0, 2), (1, 2))),
        "up_weight": normal_values(splits[9], (D, FF), D ** -0.5, 0.125, ((0, 2), (1, 2))),
        "down_weight": normal_values(splits[10], (FF, D), FF ** -0.5, 0.078125, ((0, 2), (1, 2))),
        "out_grad": normal_values(splits[11], (TOKENS, D), 1.0, 6.0, ((0, 16), (1, 2))),
    }


EPSILON = 1e-05
MASKED = -1e+30

@jax.custom_vjp
def low(v):
    return lax.optimization_barrier(v.astype(jnp.bfloat16)).astype(jnp.float32)

@jax.custom_vjp
def low_back(v):
    return v

def low_keep(v):
    return (low(v), None)

def low_pass(kept, grad):
    return (grad,)

def back_keep(v):
    return (v, None)

def back_low(kept, grad):
    return (low(grad),)
low.defvjp(low_keep, low_pass)
low_back.defvjp(back_keep, back_low)

def matmul(left, right):
    return jnp.dot(left, right, precision=lax.Precision.HIGHEST, preferred_element_type=jnp.float32)

def layout(lengths, count):
    ends = jnp.cumsum(lengths).astype(jnp.int32)
    starts = ends - lengths
    places = jnp.arange(count, dtype=jnp.int32)
    segment = lax.optimization_barrier(jnp.sum((places[:, None] >= ends[None, :]).astype(jnp.int32), axis=1))
    picked = (segment[:, None] == jnp.arange(lengths.shape[0], dtype=jnp.int32)[None, :]).astype(jnp.int32)
    position = places - lax.optimization_barrier(jnp.sum(picked * starts[None, :], axis=1))
    return (segment, position)

def rotary_tables(position):
    half_dim = HEAD_DIM // 2
    freq = 10000.0 ** (-2.0 * jnp.arange(half_dim, dtype=jnp.float32) / HEAD_DIM)
    angle = position.astype(jnp.float32)[:, None] * freq[None, :]
    cosine = jnp.concatenate([jnp.cos(angle), jnp.cos(angle)], axis=1)[:, None, :]
    sine = jnp.concatenate([jnp.sin(angle), jnp.sin(angle)], axis=1)[:, None, :]
    return (cosine, sine)

def rotate(values, cosine, sine):
    rows = values.shape[0]
    half_dim = HEAD_DIM // 2
    split = values.reshape(rows, -1, HEAD_DIM)
    turned = jnp.concatenate([-split[..., half_dim:], split[..., :half_dim]], axis=-1)
    return (split * cosine + turned * sine).reshape(rows, -1)

def attend_group(pieces):
    query, keys, values, segment = pieces
    per_kv = HEADS // KV_HEADS
    shaped_query = query.reshape(TOK_GROUP, KV_HEADS, per_kv, HEAD_DIM)
    shaped_keys = keys.reshape(TOK_GROUP, KV_HEADS, HEAD_DIM)
    shaped_values = values.reshape(TOK_GROUP, KV_HEADS, HEAD_DIM)
    scores = jnp.einsum('qkgd,tkd->kgqt', shaped_query, shaped_keys, precision=lax.Precision.HIGHEST) * HEAD_DIM ** (-0.5)
    scores = low_back(scores)
    places = jnp.arange(TOK_GROUP, dtype=jnp.int32)
    allowed = (segment[:, None] == segment[None, :]) & (places[:, None] >= places[None, :])
    scores = jnp.where(allowed, scores, MASKED)
    peak = lax.optimization_barrier(jnp.max(scores, axis=-1, keepdims=True))
    weights = jnp.exp(scores - peak)
    probs = weights / lax.optimization_barrier(jnp.sum(weights, axis=-1, keepdims=True))
    mixed = jnp.einsum('kgqt,tkd->qkgd', low(probs), shaped_values, precision=lax.Precision.HIGHEST)
    return mixed.reshape(TOK_GROUP, HEADS * HEAD_DIM)

def layer(segment, cosine, sine, resid, attn_gain, q_weight, k_weight, v_weight, o_weight, ffn_gain, gate_weight, up_weight, down_weight):
    normed_one = low(resid * lax.rsqrt(lax.optimization_barrier(jnp.mean(resid * resid, axis=1, keepdims=True)) + EPSILON) * attn_gain)
    query_pre = low_back(matmul(normed_one, q_weight))
    key_pre = low_back(matmul(normed_one, k_weight))
    values = low(low_back(matmul(normed_one, v_weight)))
    query = low(rotate(query_pre, cosine, sine))
    keys = low(rotate(key_pre, cosine, sine))
    groups = resid.shape[0] // TOK_GROUP
    attended = lax.map(jax.checkpoint(attend_group), (query.reshape(groups, TOK_GROUP, -1), keys.reshape(groups, TOK_GROUP, -1), values.reshape(groups, TOK_GROUP, -1), segment.reshape(groups, TOK_GROUP)))
    attended = low(low_back(attended.reshape(resid.shape[0], -1)))
    hidden_one = resid + low_back(matmul(attended, o_weight))
    normed_two = low(hidden_one * lax.rsqrt(lax.optimization_barrier(jnp.mean(hidden_one * hidden_one, axis=1, keepdims=True)) + EPSILON) * ffn_gain)
    gate = low_back(matmul(normed_two, gate_weight))
    upper = low_back(matmul(normed_two, up_weight))
    hidden = low(jax.nn.silu(gate) * upper)
    return hidden_one + low_back(matmul(hidden, down_weight))

def reference(tokens, seq_lengths, attn_gain, q_weight, k_weight, v_weight, o_weight, ffn_gain, gate_weight, up_weight, down_weight, out_grad):
    segment, position = jax.vmap(lambda lengths: layout(lengths, TOK_GROUP))(seq_lengths)
    segment = segment.reshape(-1)
    cosine, sine = rotary_tables(position.reshape(-1))
    floats = (tokens.astype(jnp.float32), attn_gain, q_weight.astype(jnp.float32), k_weight.astype(jnp.float32), v_weight.astype(jnp.float32), o_weight.astype(jnp.float32), ffn_gain, gate_weight.astype(jnp.float32), up_weight.astype(jnp.float32), down_weight.astype(jnp.float32))
    forward = lambda *params: layer(segment, cosine, sine, *params)
    output, pullback = jax.vjp(forward, *floats)
    grads = pullback(out_grad.astype(jnp.float32))
    return (output.astype(jnp.bfloat16), grads[0].astype(jnp.bfloat16), grads[1], grads[2], grads[3], grads[4], grads[5], grads[6], grads[7], grads[8], grads[9])
```

```python
import jax
import jax.numpy as jnp
from jax import lax
from jax.sharding import PartitionSpec as P

D = 2048
HEAD_DIM = 64

EPSILON = 1e-05
MASKED = -1e30
BF = jnp.bfloat16
F32 = jnp.float32


def dot(left, right):
    return jnp.dot(left, right, preferred_element_type=F32)


def dot_t(left, right):
    return lax.dot_general(left, right, (((1,), (1,)), ((), ())), preferred_element_type=F32)


def outer(left, right):
    return lax.dot_general(left, right, (((0,), (0,)), ((), ())), preferred_element_type=F32)


def swap(value, axis):
    return lax.ppermute(value, axis, [(0, 1), (1, 0)])


def ordered(own, other, index, axis):
    return jnp.where(
        index == 0,
        jnp.concatenate([own, other], axis=axis),
        jnp.concatenate([other, own], axis=axis),
    )


def layout(lengths, places):
    ends = jnp.cumsum(lengths)
    starts = ends - lengths
    segment = jnp.sum((places[:, None] >= ends[None, :]).astype(jnp.int32), axis=1)
    picked = (segment[:, None] == jnp.arange(lengths.shape[0], dtype=jnp.int32)[None, :]).astype(
        jnp.int32
    )
    position = places - jnp.sum(picked * starts[None, :], axis=1)
    return (segment, position)


def rotary_tables(position):
    half_dim = HEAD_DIM // 2
    freq = 10000.0 ** (-2.0 * jnp.arange(half_dim, dtype=F32) / HEAD_DIM)
    angle = position.astype(F32)[:, None] * freq[None, :]
    cosine = jnp.concatenate([jnp.cos(angle), jnp.cos(angle)], axis=1)
    sine = jnp.concatenate([jnp.sin(angle), jnp.sin(angle)], axis=1)
    return (cosine, sine)


def half_mask(width):
    return (jnp.arange(width) % HEAD_DIM < HEAD_DIM // 2)[None, :]


def rotate(values, cosine, sine):
    half_dim = HEAD_DIM // 2
    width = values.shape[1]
    times = width // HEAD_DIM
    turned = jnp.where(
        half_mask(width), -jnp.roll(values, -half_dim, axis=1), jnp.roll(values, half_dim, axis=1)
    )
    return values * jnp.tile(cosine, (1, times)) + turned * jnp.tile(sine, (1, times))


def rotate_back(grads, cosine, sine):
    half_dim = HEAD_DIM // 2
    width = grads.shape[1]
    times = width // HEAD_DIM
    turned = grads * jnp.tile(sine, (1, times))
    moved = jnp.where(
        half_mask(width), jnp.roll(turned, -half_dim, axis=1), -jnp.roll(turned, half_dim, axis=1)
    )
    return grads * jnp.tile(cosine, (1, times)) + moved


def attend(query, keys, values, allowed):
    rows = query.shape[0]
    shaped_query = query.reshape(rows, -1, HEAD_DIM)
    scores = jnp.einsum("qgd,td->gqt", shaped_query, keys, preferred_element_type=F32)
    scores = jnp.where(allowed, scores * HEAD_DIM ** (-0.5), MASKED)
    peak = jnp.max(scores, axis=-1, keepdims=True)
    weights = jnp.exp(scores - peak)
    totals = jnp.sum(weights, axis=-1, keepdims=True)
    probs = (weights / totals).astype(BF)
    logs = peak[..., 0] + jnp.log(totals[..., 0])
    mixed = jnp.einsum("gqt,td->qgd", probs, values, preferred_element_type=F32)
    return (mixed.reshape(rows, -1).astype(BF), logs)


def attend_back(query, keys, values, allowed, logs, grads):
    rows = query.shape[0]
    shaped_query = query.reshape(rows, -1, HEAD_DIM)
    shaped_grads = grads.reshape(rows, -1, HEAD_DIM)
    scale = HEAD_DIM ** (-0.5)
    scores = jnp.einsum("qgd,td->gqt", shaped_query, keys, preferred_element_type=F32)
    scores = jnp.where(allowed, scores * scale, MASKED)
    probs = jnp.exp(scores - logs[:, :, None])
    grad_probs = jnp.einsum("qgd,td->gqt", shaped_grads, values, preferred_element_type=F32)
    centred = grad_probs - jnp.sum(probs * grad_probs, axis=-1, keepdims=True)
    grad_scores = (probs * centred).astype(BF)
    grad_query = jnp.einsum("gqt,td->qgd", grad_scores, keys, preferred_element_type=F32) * scale
    grad_keys = (
        jnp.einsum("gqt,qgd->td", grad_scores, shaped_query, preferred_element_type=F32) * scale
    )
    grad_values = jnp.einsum(
        "gqt,qgd->td", probs.astype(BF), shaped_grads, preferred_element_type=F32
    )
    return (grad_query.reshape(rows, -1), grad_keys, grad_values)


def pair_exchange(parts, size, pair):
    sent = lax.dynamic_index_in_dim(parts, 1 - pair, 2, keepdims=False)
    kept = lax.dynamic_index_in_dim(parts, pair, 2, keepdims=False)
    moved = lax.ppermute(sent, "dp", [(i, i ^ 1) for i in range(size)])
    return (kept.astype(F32) + moved.astype(F32)).astype(BF)


def line_reduce(parts, lines, place):
    def piece(index):
        return lax.dynamic_index_in_dim(
            parts, jnp.clip(index, 0, lines - 1), 1, keepdims=False
        )

    right = left = None
    for step in range(1, lines):
        going_right = piece(lines - step + place)
        going_left = piece(step + place - lines)
        if right is not None:
            going_right = (going_right.astype(F32) + right.astype(F32)).astype(BF)
            going_left = (going_left.astype(F32) + left.astype(F32)).astype(BF)
        sources = range(min(step, lines - 1))
        right = lax.ppermute(
            going_right,
            "dp",
            [(2 * z + x, 2 * z + 2 + x) for z in sources for x in range(2)],
        )
        left = lax.ppermute(
            going_left,
            "dp",
            [
                (2 * (lines - 1 - z) + x, 2 * (lines - 2 - z) + x)
                for z in sources
                for x in range(2)
            ],
        )
    total = piece(place).astype(F32)
    if right is not None:
        total = total + right.astype(F32) + left.astype(F32)
    return total


def dp_reduce(block):
    size = lax.axis_size("dp")
    place = lax.axis_index("dp")
    lead, rows, cols = block.shape
    parts = block.reshape(lead, size // 2, 2, rows // size, cols)
    paired = pair_exchange(parts, size, place % 2)
    return line_reduce(paired, size // 2, place // 2)


def small_total(value):
    value = value + swap(value, "row")
    size = lax.axis_size("dp")
    bit = 1
    while bit < size:
        value = value + lax.ppermute(value, "dp", [(i, i ^ bit) for i in range(size)])
        bit *= 2
    return value


def shards(
    tokens,
    seq_lengths,
    attn_gain,
    q_weight,
    k_weight,
    v_weight,
    o_weight,
    ffn_gain,
    gate_weight,
    up_weight,
    down_weight,
    out_grad,
):
    row = lax.axis_index("row")
    col = lax.axis_index("col")
    rows = tokens.shape[0]
    group = 2 * rows
    q_half = q_weight.shape[1] // 2
    k_half = k_weight.shape[1] // 2
    f_half = gate_weight.shape[1] // 2

    def part(value, index, size, axis):
        return lax.dynamic_slice_in_dim(value, index * size, size, axis)

    tokens_row = swap(tokens, "row")
    grad_row = swap(out_grad, "row")

    def qkv_part(index):
        return jnp.concatenate(
            [
                part(q_weight, index, q_half, 1),
                part(k_weight, index, k_half, 1),
                part(v_weight, index, k_half, 1),
            ],
            axis=1,
        )

    qkv_own = qkv_part(col)
    qkv_recv = swap(qkv_part(1 - col), "col")
    gate_own = part(gate_weight, col, f_half, 1)
    gate_recv = swap(part(gate_weight, 1 - col, f_half, 1), "col")
    up_own = part(up_weight, col, f_half, 1)
    up_recv = swap(part(up_weight, 1 - col, f_half, 1), "col")
    down_own = part(down_weight, col, f_half, 0)
    down_other = part(down_weight, 1 - col, f_half, 0)
    down_recv = swap(down_other, "col")
    qkv_full = jnp.concatenate([q_weight, k_weight, v_weight], axis=1)

    places = (jnp.arange(group, dtype=jnp.int32) + row * rows) % group
    segment, position = layout(seq_lengths[0], places)
    cosine, sine = rotary_tables(position)
    allowed = (segment[:, None] == segment[None, :]) & (places[:, None] >= places[None, :])

    both = jnp.concatenate([tokens, tokens_row], axis=0)
    resid = both.astype(F32)
    scaled_one = (resid * attn_gain).astype(BF)
    squares = jnp.sum(resid * resid, axis=1)
    squares = squares + swap(squares, "col")
    inverse_one = lax.rsqrt(squares / D + EPSILON)
    scaled_one_other = swap(scaled_one, "col")
    qkv = (dot(scaled_one, qkv_own) + dot(scaled_one_other, qkv_recv)) * inverse_one[:, None]
    query = rotate(qkv[:, :q_half], cosine, sine).astype(BF)
    keys = rotate(qkv[:, q_half : q_half + k_half], cosine, sine).astype(BF)
    values = qkv[:, q_half + k_half :].astype(BF)
    attended, logs = attend(query, keys, values, allowed)
    attended_other = swap(attended, "col")
    o_own = part(o_weight, col, q_half, 0)
    o_other = part(o_weight, 1 - col, q_half, 0)
    partial = dot(attended, o_own) + dot(attended_other, o_other)
    sent = partial.astype(BF)
    partial_own = swap(sent[rows:], "row")
    partial_other = swap(sent[:rows], "row")
    hidden_one = resid + partial + jnp.concatenate([partial_own, partial_other], axis=0).astype(F32)
    scaled_two = (hidden_one * ffn_gain).astype(BF)
    squares_two = jnp.sum(hidden_one * hidden_one, axis=1)
    squares_two = squares_two + swap(squares_two, "col")
    inverse_two = lax.rsqrt(squares_two / D + EPSILON)[:, None]
    scaled_two_other = swap(scaled_two, "col")

    grad_two = jnp.concatenate([out_grad, grad_row], axis=0)
    grad_two_other = swap(grad_two, "col")
    grad_hidden = dot_t(grad_two, down_own) + dot_t(grad_two_other, down_recv)

    gate = (dot(scaled_two, gate_own) + dot(scaled_two_other, gate_recv)) * inverse_two
    upper = (dot(scaled_two, up_own) + dot(scaled_two_other, up_recv)) * inverse_two
    sigmoid_gate = jax.nn.sigmoid(gate)
    activated = gate * sigmoid_gate
    hidden = (activated * upper).astype(BF)
    grad_gate = (
        grad_hidden * upper * sigmoid_gate * (1.0 + gate * (1.0 - sigmoid_gate)) * inverse_two
    ).astype(BF)
    grad_up = (grad_hidden * activated * inverse_two).astype(BF)
    hidden_other = swap(hidden, "col")

    back_other = (dot_t(grad_gate, gate_recv) + dot_t(grad_up, up_recv)).astype(BF)
    back_moved = swap(back_other, "col")
    back = dot_t(grad_gate, gate_own) + dot_t(grad_up, up_own) + back_moved.astype(F32)
    back_sent = back.astype(BF)
    back_own_row = swap(back_sent[rows:], "row")
    back_other_row = swap(back_sent[:rows], "row")

    hidden_full = ordered(hidden, hidden_other, col, 1)
    grad_down_weight = outer(hidden_full, grad_two).astype(BF)
    down_sum = dp_reduce(grad_down_weight[None])[0]
    grad_gate_up = jnp.concatenate([grad_gate, grad_up], axis=1)
    gate_up_blocks = jnp.stack(
        [outer(scaled_two, grad_gate_up), outer(scaled_two_other, grad_gate_up)]
    ).astype(BF)
    gate_up_sum = dp_reduce(gate_up_blocks)
    gate_up_moved = swap(gate_up_sum[1].astype(BF), "col").astype(F32)
    gate_sum = ordered(gate_up_sum[0][:, :f_half], gate_up_moved[:, :f_half], col, 1)
    up_sum = ordered(gate_up_sum[0][:, f_half:], gate_up_moved[:, f_half:], col, 1)

    down_partial = dot(hidden, down_own) + dot(hidden_other, down_other)
    down_moved = swap(down_partial[rows:].astype(BF), "row")
    result = (hidden_one[:rows] + down_partial[:rows] + down_moved.astype(F32)).astype(BF)

    back = back + jnp.concatenate([back_own_row, back_other_row], axis=0).astype(F32)
    gain_two = small_total(jnp.sum(back[:rows] * hidden_one[:rows], axis=0))
    scaled_back = back * ffn_gain
    inner = jnp.sum(scaled_back * hidden_one, axis=1)
    inner = inner + swap(inner, "col")
    grad_one = (
        grad_two.astype(F32)
        + scaled_back
        - hidden_one * (inverse_two[:, 0] ** 2 * inner / D)[:, None]
    )
    branch = grad_one.astype(BF)
    grad_attended = swap(dot_t(branch, o_other).astype(BF), "col").astype(F32) + dot_t(
        branch, o_own
    )
    attended_full = ordered(attended, attended_other, col, 1)
    grad_o_weight = outer(attended_full, branch).astype(BF)
    o_sum = dp_reduce(grad_o_weight[None])[0]

    grad_query, grad_keys, grad_values = attend_back(
        query, keys, values, allowed, logs, grad_attended.astype(BF)
    )
    grad_qkv = (
        jnp.concatenate(
            [
                rotate_back(grad_query, cosine, sine),
                rotate_back(grad_keys, cosine, sine),
                grad_values,
            ],
            axis=1,
        )
        * inverse_one[:, None]
    ).astype(BF)
    grad_qkv_other = swap(grad_qkv, "col")

    def pick(start, size):
        return ordered(
            grad_qkv[:, start : start + size], grad_qkv_other[:, start : start + size], col, 1
        )

    grad_qkv_full = jnp.concatenate(
        [pick(0, q_half), pick(q_half, k_half), pick(q_half + k_half, k_half)], axis=1
    )
    qkv_sum = dp_reduce(outer(scaled_one, grad_qkv_full).astype(BF)[None])[0]
    last = dot_t(grad_qkv_full, qkv_full)
    last_moved = swap(last[rows:].astype(BF), "row")
    gain_one = small_total(jnp.sum(last * resid, axis=0))
    last = last[:rows] + last_moved.astype(F32)
    scaled_last = last * attn_gain
    own = tokens.astype(F32)
    inner_one = jnp.sum(scaled_last * own, axis=1)
    inner_one = inner_one + swap(inner_one, "col")
    grad_tokens = (
        grad_one[:rows]
        + scaled_last
        - own * (inverse_one[:rows] ** 2 * inner_one / D)[:, None]
    ).astype(BF)
    q_cols, k_cols = 2 * q_half, 2 * k_half
    return (
        result,
        grad_tokens,
        gain_one,
        qkv_sum[:, :q_cols],
        qkv_sum[:, q_cols : q_cols + k_cols],
        qkv_sum[:, q_cols + k_cols :],
        o_sum,
        gain_two,
        gate_sum,
        up_sum,
        down_sum,
    )


def solution(mesh):
    placed = (
        P(("dp", "row"), "col"),
        P("dp", None),
        P("col"),
        P("col", "row"),
        P("col", "row"),
        P("col", "row"),
        P("row", "col"),
        P("col"),
        P("col", "row"),
        P("col", "row"),
        P("row", "col"),
        P(("dp", "row"), "col"),
    )
    return jax.shard_map(
        shards,
        mesh=mesh,
        in_specs=placed,
        out_specs=(
            P(("dp", "row"), "col"),
            P(("dp", "row"), "col"),
            P("col"),
            P(("col", "dp"), "row"),
            P(("col", "dp"), "row"),
            P(("col", "dp"), "row"),
            P(("row", "dp"), "col"),
            P("col"),
            P(("col", "dp"), "row"),
            P(("col", "dp"), "row"),
            P(("row", "dp"), "col"),
        ),
        check_vma=False,
    )
```

```python
import functools

import jax
import jax.numpy as jnp
from jax import lax
from jax.experimental import pallas as pl
from jax.experimental.pallas import tpu as pltpu
from jax.sharding import PartitionSpec as P

D = 2048
HEAD_DIM = 64

EPSILON = 1e-05
MASKED = -1e30
BF = jnp.bfloat16
F32 = jnp.float32


def dot(left, right):
    return jnp.dot(left, right, preferred_element_type=F32)


def dot_t(left, right):
    return lax.dot_general(left, right, (((1,), (1,)), ((), ())), preferred_element_type=F32)


def outer(left, right):
    return lax.dot_general(left, right, (((0,), (0,)), ((), ())), preferred_element_type=F32)


def swap(value, axis):
    return lax.ppermute(value, axis, [(0, 1), (1, 0)])


def ordered(own, other, index, axis):
    return jnp.where(
        index == 0,
        jnp.concatenate([own, other], axis=axis),
        jnp.concatenate([other, own], axis=axis),
    )


def layout(lengths, places):
    ends = jnp.cumsum(lengths)
    starts = ends - lengths
    segment = jnp.sum((places[:, None] >= ends[None, :]).astype(jnp.int32), axis=1)
    picked = (segment[:, None] == jnp.arange(lengths.shape[0], dtype=jnp.int32)[None, :]).astype(
        jnp.int32
    )
    return jnp.sum(picked * starts[None, :], axis=1)


def rotary_tables(position):
    half_dim = HEAD_DIM // 2
    freq = 10000.0 ** (-2.0 * jnp.arange(half_dim, dtype=F32) / HEAD_DIM)
    angle = freq[:, None] * position.astype(F32)[None, :]
    return (jnp.cos(angle), jnp.sin(angle))


QUERY_BLOCK = 256
HALF = HEAD_DIM // 2
VMEM_BYTES = 56 * 1024 * 1024


def write_bias(bias, start):
    group = bias.shape[0]
    for block in range(group // QUERY_BLOCK):
        first = block * QUERY_BLOCK
        last = first + QUERY_BLOCK
        key = lax.broadcasted_iota(jnp.int32, (last, QUERY_BLOCK), 0)
        query = first + lax.broadcasted_iota(jnp.int32, (last, QUERY_BLOCK), 1)
        allowed = (key <= query) & (key >= start[:, first:last])
        bias[:last, first:last] = jnp.where(allowed, 0.0, MASKED)


def attend_kernel(
    row, own, other, own_weight, other_weight, inverse, cosine, sine, start,
    query_out, key_out, value_out, logs_out, mixed_out, pre, key_rows, bias, mixed,
):
    group = own.shape[0]
    half = group // 2
    heads = query_out.shape[0] // HEAD_DIM
    first = pl.multiple_of(row[0] * half, 128)
    second = pl.multiple_of((1 - row[0]) * half, 128)
    chunk = own_weight.shape[0] // 2

    def project(index, carry):
        place = pl.ds(pl.multiple_of(index * chunk, 64), chunk)
        total = dot_t(own_weight[place, :], own[...]) + dot_t(other_weight[place, :], other[...])
        total = total * inverse[...]
        pre[place, pl.ds(first, half)] = total[:, :half]
        pre[place, pl.ds(second, half)] = total[:, half:]
        return carry

    lax.fori_loop(0, 2, project, 0)
    write_bias(bias, start)

    def turned(base):
        low = pre[pl.ds(base, HALF), :]
        high = pre[pl.ds(base + HALF, HALF), :]
        cos, sin = cosine[...], sine[...]
        return jnp.concatenate([low * cos - high * sin, high * cos + low * sin], axis=0)

    keys = turned(heads * HEAD_DIM).astype(BF)
    key_out[...] = keys
    key_rows[...] = keys.astype(F32).T.astype(BF)
    value_out[...] = pre[(heads + 1) * HEAD_DIM :, :].astype(BF)

    def head(index, carry):
        base = pl.multiple_of(index * HEAD_DIM, HEAD_DIM)
        place = pl.ds(base, HEAD_DIM)
        query_out[place, :] = (turned(base).astype(BF).astype(F32) * HEAD_DIM ** (-0.5)).astype(BF)
        for block in range(group // QUERY_BLOCK):
            low = block * QUERY_BLOCK
            high = low + QUERY_BLOCK
            scores = dot(key_rows[:high, :], query_out[place, low:high]) + bias[:high, low:high]
            peak = jnp.max(scores, axis=0, keepdims=True)
            weights = jnp.exp(scores - peak)
            totals = jnp.sum(weights, axis=0, keepdims=True)
            probs = (weights * (1.0 / totals)).astype(BF)
            mixed[place, low:high] = dot(value_out[:, :high], probs)
            logs_out[pl.ds(index, 1), low:high] = peak + jnp.log(totals)
        return carry

    lax.fori_loop(0, heads, head, 0)
    mixed_out[:, :half] = mixed[:, pl.ds(first, half)].astype(BF)
    mixed_out[:, half:] = mixed[:, pl.ds(second, half)].astype(BF)


def in_vmem(count):
    return [pl.BlockSpec(memory_space=pltpu.VMEM)] * count


def attend(row, own, other, own_weight, other_weight, inverse, cosine, sine, start):
    group = own.shape[0]
    width = own_weight.shape[0]
    wide = width - 2 * HEAD_DIM
    heads = wide // HEAD_DIM
    cost = 4 * width * own.shape[1] * group + 3 * heads * group * group * HEAD_DIM
    return pl.pallas_call(
        attend_kernel,
        out_shape=(
            jax.ShapeDtypeStruct((wide, group), BF),
            jax.ShapeDtypeStruct((HEAD_DIM, group), BF),
            jax.ShapeDtypeStruct((HEAD_DIM, group), BF),
            jax.ShapeDtypeStruct((heads, group), F32),
            jax.ShapeDtypeStruct((wide, group), BF),
        ),
        in_specs=[pl.BlockSpec(memory_space=pltpu.SMEM)] + in_vmem(8),
        out_specs=tuple(in_vmem(5)),
        scratch_shapes=[
            pltpu.VMEM((width, group), F32),
            pltpu.VMEM((group, HEAD_DIM), BF),
            pltpu.VMEM((group, group), F32),
            pltpu.VMEM((wide, group), F32),
        ],
        compiler_params=pltpu.CompilerParams(vmem_limit_bytes=VMEM_BYTES),
        cost_estimate=pl.CostEstimate(
            flops=2 * cost, bytes_accessed=10**7, transcendentals=heads * group * group
        ),
        name="attend",
    )(row, own, other, own_weight, other_weight, inverse, cosine, sine, start)


def attend_back_kernel(
    row, query, key, value, logs, grad, inverse, cosine, sine, start,
    grad_out, key_rows, value_rows, bias, grads, grad_query, grad_key, grad_value,
):
    group = query.shape[1]
    half = group // 2
    heads = query.shape[0] // HEAD_DIM
    first = pl.multiple_of(row[0] * half, 128)
    second = pl.multiple_of((1 - row[0]) * half, 128)
    grads[:, pl.ds(first, half)] = grad[:, :half]
    grads[:, pl.ds(second, half)] = grad[:, half:]
    write_bias(bias, start)
    key_rows[...] = key[...].astype(F32).T.astype(BF)
    value_rows[...] = value[...].astype(F32).T.astype(BF)
    grad_key[...] = jnp.zeros_like(grad_key)
    grad_value[...] = jnp.zeros_like(grad_value)
    cos, sin = cosine[...], sine[...]

    def turned_back(full):
        low, high = full[:HALF], full[HALF:]
        return jnp.concatenate([low * cos + high * sin, high * cos - low * sin], axis=0)

    def head(index, carry):
        place = pl.ds(pl.multiple_of(index * HEAD_DIM, HEAD_DIM), HEAD_DIM)
        for block in range(group // QUERY_BLOCK):
            low = block * QUERY_BLOCK
            high = low + QUERY_BLOCK
            queries = query[place, low:high]
            outs = grads[place, low:high]
            scores = dot(key_rows[:high, :], queries) + bias[:high, low:high]
            probs = jnp.exp(scores - logs[pl.ds(index, 1), low:high])
            grad_probs = probs * dot(value_rows[:high, :], outs)
            total = jnp.sum(grad_probs, axis=0, keepdims=True)
            grad_scores = (grad_probs - probs * total).astype(BF)
            grad_query[place, low:high] = dot(key[:, :high], grad_scores) * HEAD_DIM ** (-0.5)
            grad_key[:high, :] += dot_t(grad_scores, queries)
            grad_value[:high, :] += dot_t(probs.astype(BF), outs)
        grad_query[place, :] = turned_back(grad_query[place, :])
        return carry

    lax.fori_loop(0, heads, head, 0)
    wide = heads * HEAD_DIM
    grad_query[wide : wide + HEAD_DIM, :] = turned_back(grad_key[...].T)
    grad_query[wide + HEAD_DIM :, :] = grad_value[...].T
    scale = inverse[...]
    grad_out[:, :half] = (grad_query[:, pl.ds(first, half)] * scale[:, :half]).astype(BF)
    grad_out[:, half:] = (grad_query[:, pl.ds(second, half)] * scale[:, half:]).astype(BF)


def attend_back(row, query, key, value, logs, grad, inverse, cosine, sine, start):
    wide, group = query.shape
    heads = wide // HEAD_DIM
    width = wide + 2 * HEAD_DIM
    cost = 10 * heads * group * group * HEAD_DIM
    return pl.pallas_call(
        attend_back_kernel,
        out_shape=jax.ShapeDtypeStruct((width, group), BF),
        in_specs=[pl.BlockSpec(memory_space=pltpu.SMEM)] + in_vmem(9),
        out_specs=in_vmem(1)[0],
        scratch_shapes=[
            pltpu.VMEM((group, HEAD_DIM), BF),
            pltpu.VMEM((group, HEAD_DIM), BF),
            pltpu.VMEM((group, group), F32),
            pltpu.VMEM((wide, group), BF),
            pltpu.VMEM((width, group), F32),
            pltpu.VMEM((group, HEAD_DIM), F32),
            pltpu.VMEM((group, HEAD_DIM), F32),
        ],
        compiler_params=pltpu.CompilerParams(vmem_limit_bytes=VMEM_BYTES),
        cost_estimate=pl.CostEstimate(
            flops=4 * cost, bytes_accessed=5 * 10**6, transcendentals=heads * group * group
        ),
        name="attend_back",
    )(row, query, key, value, logs, grad, inverse, cosine, sine, start)


def interleave_kernel(index, first, second, out):
    lane = first.shape[1]
    out[:, :lane] = first[...]
    out[:, lane:] = second[...]


def interleave(index, first, second):
    depth, whole = first.shape
    tiles = whole // 2 // 128
    spec = pl.BlockSpec((depth, 128), lambda step, place: (0, place[0] * tiles + step))
    return pl.pallas_call(
        interleave_kernel,
        out_shape=jax.ShapeDtypeStruct((depth, whole), first.dtype),
        grid_spec=pltpu.PrefetchScalarGridSpec(
            num_scalar_prefetch=1,
            grid=(tiles,),
            in_specs=[spec, spec],
            out_specs=pl.BlockSpec((depth, 256), lambda step, place: (0, step)),
        ),
        cost_estimate=pl.CostEstimate(
            flops=0, bytes_accessed=4 * depth * whole, transcendentals=0
        ),
        name="interleave",
    )(index, first, second)


def ffn_kernel(own, other, own_weight, other_weight, grad, inverse, hidden_out, grad_out):
    rows = own.shape[0] // 2
    for block in range(2):
        place = slice(block * rows, (block + 1) * rows)
        both = dot(own[place, :], own_weight[...]) + dot(other[place, :], other_weight[...])
        scale = inverse[place, :]
        both = both * scale
        gate, up = both[:, :128], both[:, 128:]
        sigmoid = 1.0 / (1.0 + jnp.exp(-gate))
        active = gate * sigmoid
        hidden_out[place, :] = (active * up).astype(BF)
        back = grad[place, :].astype(F32) * scale
        grad_out[place, :128] = (back * up * sigmoid * (1.0 + gate * (1.0 - sigmoid))).astype(BF)
        grad_out[place, 128:] = (back * active).astype(BF)


def ffn(own, other, own_weight, other_weight, grad, inverse):
    group, depth = own.shape
    wide = own_weight.shape[1]
    tiles = wide // 256
    return pl.pallas_call(
        ffn_kernel,
        out_shape=(
            jax.ShapeDtypeStruct((group, wide // 2), BF),
            jax.ShapeDtypeStruct((group, wide), BF),
        ),
        grid=(tiles,),
        in_specs=[
            pl.BlockSpec((group, depth), lambda step: (0, 0)),
            pl.BlockSpec((group, depth), lambda step: (0, 0)),
            pl.BlockSpec((depth, 256), lambda step: (0, step)),
            pl.BlockSpec((depth, 256), lambda step: (0, step)),
            pl.BlockSpec((group, 128), lambda step: (0, step)),
            pl.BlockSpec((group, 1), lambda step: (0, 0)),
        ],
        out_specs=(
            pl.BlockSpec((group, 128), lambda step: (0, step)),
            pl.BlockSpec((group, 256), lambda step: (0, step)),
        ),
        compiler_params=pltpu.CompilerParams(vmem_limit_bytes=VMEM_BYTES),
        cost_estimate=pl.CostEstimate(
            flops=4 * group * depth * wide,
            bytes_accessed=4 * depth * wide + 10 * group * wide,
            transcendentals=group * wide,
        ),
        name="ffn",
    )(own, other, own_weight, other_weight, grad, inverse)


def separate(value):
    tiles = range(value.shape[1] // 128)
    parts = [value[:, tile * 128 : (tile + 1) * 128] for tile in tiles]
    return (jnp.concatenate(parts[0::2], axis=1), jnp.concatenate(parts[1::2], axis=1))


def add_low(one, two):
    return (one.astype(F32) + two.astype(F32)).astype(BF)


def pair_exchange(parts, axis):
    size = lax.axis_size("dp")
    pair = lax.axis_index("dp") % 2
    sent = lax.dynamic_index_in_dim(parts, 1 - pair, axis, keepdims=False)
    kept = lax.dynamic_index_in_dim(parts, pair, axis, keepdims=False)
    moved = lax.ppermute(sent.astype(BF), "dp", [(i, i ^ 1) for i in range(size)])
    return kept.astype(F32) + moved.astype(F32)


def line_reduce(piece):
    lines = lax.axis_size("dp") // 2
    place = lax.axis_index("dp") // 2
    right = left = None
    for step in range(1, lines):
        going_right = piece(jnp.clip(lines - step + place, 0, lines - 1))
        going_left = piece(jnp.clip(step + place - lines, 0, lines - 1))
        if right is not None:
            going_right = add_low(going_right, right)
            going_left = add_low(going_left, left)
        sources = [(z, x) for z in range(min(step, lines - 1)) for x in range(2)]
        last = lines - 1
        right = lax.ppermute(going_right, "dp", [(2 * z + x, 2 * z + 2 + x) for z, x in sources])
        left = lax.ppermute(
            going_left, "dp", [(2 * (last - z) + x, 2 * (last - z) - 2 + x) for z, x in sources]
        )
    total = piece(place).astype(F32)
    if right is not None:
        total = total + right.astype(F32) + left.astype(F32)
    return total


def own_first(lines, col):
    half = lines // 2
    return lambda z: ((z // half) ^ col) * half + z % half


def plain(z):
    return z


def pairs_then_line(block, lead, place):
    size = lax.axis_size("dp")
    rows = block.shape[0] // (lead * size)
    parts = block.reshape(lead, size // 2, 2, rows, block.shape[1])
    paired = pair_exchange(parts, 2).astype(BF)
    return line_reduce(
        lambda z: lax.dynamic_index_in_dim(paired, place(z), 1, keepdims=False)
    )


def line_then_pairs(block, place):
    size = lax.axis_size("dp")
    parts = block.reshape(size // 2, 2, block.shape[0] // size, block.shape[1])
    total = line_reduce(lambda z: lax.dynamic_index_in_dim(parts, place(z), 0, keepdims=False))
    return pair_exchange(total, 0)


def everyone(value):
    return jnp.sum(lax.all_gather(value, ("dp", "row")), axis=0)


def shards(
    tokens,
    seq_lengths,
    attn_gain,
    q_weight,
    k_weight,
    v_weight,
    o_weight,
    ffn_gain,
    gate_weight,
    up_weight,
    down_weight,
    out_grad,
):
    row = lax.axis_index("row")
    col = lax.axis_index("col")
    rows = tokens.shape[0]
    group = 2 * rows
    q_half = q_weight.shape[1] // 2
    k_half = k_weight.shape[1] // 2
    f_half = gate_weight.shape[1] // 2
    lines = lax.axis_size("dp") // 2

    def part(value, index, size, axis):
        return lax.dynamic_slice_in_dim(value, index * size, size, axis)

    tokens_row = swap(tokens, "row")

    def qkv_part(index):
        return jnp.concatenate(
            [
                part(q_weight, index, q_half, 1),
                part(k_weight, index, k_half, 1),
                part(v_weight, index, k_half, 1),
            ],
            axis=1,
        ).T

    qkv_other = qkv_part(1 - col)
    qkv_recv = swap(qkv_other, "col")
    qkv_own = qkv_part(col)
    wide_other = interleave((1 - col)[None], gate_weight, up_weight)
    wide_recv = swap(wide_other, "col")
    wide_own = interleave(col[None], gate_weight, up_weight)
    down_own = part(down_weight, col, f_half, 0)
    down_other = part(down_weight, 1 - col, f_half, 0)
    down_recv = swap(down_other, "col")

    places = jnp.arange(group, dtype=jnp.int32)
    start = layout(seq_lengths[0], places)
    cosine, sine = rotary_tables(places - start)
    start = start[None, :]
    which = row[None]

    tokens_row, late_grad = lax.optimization_barrier((tokens_row, out_grad))
    grad_row = swap(late_grad, "row")
    both = jnp.concatenate([tokens, tokens_row], axis=0)
    resid = both.astype(F32)
    scaled_one = (resid * attn_gain).astype(BF)
    squares = jnp.sum(resid * resid, axis=1)
    squares = squares + swap(squares, "col")
    inverse_one = lax.rsqrt(squares / D + EPSILON)
    scaled_one_other = swap(scaled_one, "col")
    query, keys, values, logs, mixed = attend(
        which,
        scaled_one,
        scaled_one_other,
        qkv_own,
        qkv_recv,
        inverse_one[None, :],
        cosine,
        sine,
        start,
    )
    mixed_other = swap(mixed, "col")
    o_own = part(o_weight, col, q_half, 0)
    o_other = part(o_weight, 1 - col, q_half, 0)
    partial = outer(mixed, o_own) + outer(mixed_other, o_other)
    sent = partial.astype(BF)
    partial_own = swap(sent[rows:], "row")
    partial_other = swap(sent[:rows], "row")

    grad_two = jnp.concatenate([out_grad, grad_row], axis=0)
    grad_two_other = swap(grad_two, "col")
    grad_hidden = (dot_t(grad_two, down_own) + dot_t(grad_two_other, down_recv)).astype(BF)

    hidden_one = resid + partial + jnp.concatenate([partial_own, partial_other], axis=0).astype(F32)
    scaled_two = (hidden_one * ffn_gain).astype(BF)
    squares_two = jnp.sum(hidden_one * hidden_one, axis=1)
    squares_two = squares_two + swap(squares_two, "col")
    inverse_two = lax.rsqrt(squares_two / D + EPSILON)
    scaled_two_other = swap(scaled_two, "col")
    hidden, grad_wide = ffn(
        scaled_two, scaled_two_other, wide_own, wide_recv, grad_hidden, inverse_two[:, None]
    )
    hidden_other = swap(hidden, "col")

    back_other = dot_t(grad_wide, wide_recv).astype(BF)
    back_moved = swap(back_other, "col")
    back = dot_t(grad_wide, wide_own) + back_moved.astype(F32)
    back_sent = back.astype(BF)
    back_own_row = swap(back_sent[rows:], "row")
    back_other_row = swap(back_sent[:rows], "row")

    hidden_both = jnp.concatenate([hidden, hidden_other], axis=1)
    down_sum = line_then_pairs(outer(hidden_both, grad_two).astype(BF), own_first(lines, col))
    scaled_both = jnp.concatenate([scaled_two, scaled_two_other], axis=1)
    wide_sum = pairs_then_line(outer(scaled_both, grad_wide).astype(BF), 2, plain)
    gate_own, up_own = separate(wide_sum[0])
    gate_other, up_other = separate(swap(wide_sum[1].astype(BF), "col").astype(F32))
    gate_sum = ordered(gate_own, gate_other, col, 1)
    up_sum = ordered(up_own, up_other, col, 1)

    down_partial = dot(hidden, down_own) + dot(hidden_other, down_other)
    down_moved = swap(down_partial[rows:].astype(BF), "row")
    result = (hidden_one[:rows] + down_partial[:rows] + down_moved.astype(F32)).astype(BF)

    back = back + jnp.concatenate([back_own_row, back_other_row], axis=0).astype(F32)
    gain_two = everyone(jnp.sum(back[:rows] * hidden_one[:rows], axis=0))
    scaled_back = back * ffn_gain
    inner = jnp.sum(scaled_back * hidden_one, axis=1)
    inner = inner + swap(inner, "col")
    grad_one = (
        grad_two.astype(F32) + scaled_back - hidden_one * (inverse_two**2 * inner / D)[:, None]
    )
    branch = grad_one.astype(BF)
    grad_mixed_moved = swap(dot_t(o_other, branch).astype(BF), "col")
    grad_mixed = (dot_t(o_own, branch) + grad_mixed_moved.astype(F32)).astype(BF)
    mixed_both = jnp.concatenate([mixed, mixed_other], axis=0)
    o_sum = pairs_then_line(dot(mixed_both, branch).astype(BF), 1, own_first(lines, col))[0]

    grad_qkv = attend_back(
        which,
        query,
        keys,
        values,
        logs,
        grad_mixed,
        inverse_one[None, :],
        cosine,
        sine,
        start,
    )
    grad_qkv_both = jnp.concatenate([grad_qkv, swap(grad_qkv, "col")], axis=0)
    qkv_grad = lax.dot_general(
        scaled_one, grad_qkv_both, (((0,), (1,)), ((), ())), preferred_element_type=F32
    )
    qkv_sum = pairs_then_line(qkv_grad.astype(BF), 1, plain)[0]
    last = outer(grad_qkv_both, jnp.concatenate([qkv_own, qkv_other], axis=0))
    last_moved = swap(last[rows:].astype(BF), "row")
    gain_one = everyone(jnp.sum(last * resid, axis=0))
    last = last[:rows] + last_moved.astype(F32)
    scaled_last = last * attn_gain
    own = tokens.astype(F32)
    inner_one = jnp.sum(scaled_last * own, axis=1)
    inner_one = inner_one + swap(inner_one, "col")
    grad_tokens = (
        grad_one[:rows]
        + scaled_last
        - own * (inverse_one[:rows] ** 2 * inner_one / D)[:, None]
    ).astype(BF)
    width = q_half + 2 * k_half

    def pick(first, size):
        return ordered(
            qkv_sum[:, first : first + size],
            qkv_sum[:, width + first : width + first + size],
            col,
            1,
        )

    return (
        result,
        grad_tokens,
        gain_one,
        pick(0, q_half),
        pick(q_half, k_half),
        pick(q_half + k_half, k_half),
        o_sum,
        gain_two,
        gate_sum,
        up_sum,
        down_sum,
    )


def solution(mesh):
    placed = (
        P(("dp", "row"), "col"),
        P("dp", None),
        P("col"),
        P("col", "row"),
        P("col", "row"),
        P("col", "row"),
        P("row", "col"),
        P("col"),
        P("col", "row"),
        P("col", "row"),
        P("row", "col"),
        P(("dp", "row"), "col"),
    )
    return jax.shard_map(
        shards,
        mesh=mesh,
        in_specs=placed,
        out_specs=(
            P(("dp", "row"), "col"),
            P(("dp", "row"), "col"),
            P("col"),
            P(("col", "dp"), "row"),
            P(("col", "dp"), "row"),
            P(("col", "dp"), "row"),
            P(("row", "dp"), "col"),
            P("col"),
            P(("col", "dp"), "row"),
            P(("col", "dp"), "row"),
            P(("row", "dp"), "col"),
        ),
        check_vma=False,
    )
```

```python
import functools

import jax
import jax.numpy as jnp
from jax import lax
from jax.experimental import pallas as pl
from jax.experimental.pallas import tpu as pltpu
from jax.sharding import PartitionSpec as P

D = 2048
HEAD_DIM = 64

EPSILON = 1e-05
MASKED = -1e30
BF = jnp.bfloat16
F32 = jnp.float32


def dot(left, right):
    return jnp.dot(left, right, preferred_element_type=F32)


def dot_t(left, right):
    return lax.dot_general(left, right, (((1,), (1,)), ((), ())), preferred_element_type=F32)


def outer(left, right):
    return lax.dot_general(left, right, (((0,), (0,)), ((), ())), preferred_element_type=F32)


def swap(value, axis):
    return lax.ppermute(value, axis, [(0, 1), (1, 0)])


def ordered(own, other, index, axis):
    return jnp.where(
        index == 0,
        jnp.concatenate([own, other], axis=axis),
        jnp.concatenate([other, own], axis=axis),
    )


def layout(lengths, places):
    ends = jnp.cumsum(lengths)
    starts = ends - lengths
    segment = jnp.sum((places[:, None] >= ends[None, :]).astype(jnp.int32), axis=1)
    picked = (segment[:, None] == jnp.arange(lengths.shape[0], dtype=jnp.int32)[None, :]).astype(
        jnp.int32
    )
    return jnp.sum(picked * starts[None, :], axis=1)


def rotary_tables(position):
    half_dim = HEAD_DIM // 2
    freq = 10000.0 ** (-2.0 * jnp.arange(half_dim, dtype=F32) / HEAD_DIM)
    angle = freq[:, None] * position.astype(F32)[None, :]
    return (jnp.cos(angle), jnp.sin(angle))


QUERY_BLOCK = 256
HALF = HEAD_DIM // 2
VMEM_BYTES = 56 * 1024 * 1024


def write_bias(bias, start):
    group = bias.shape[0]
    for block in range(group // QUERY_BLOCK):
        first = block * QUERY_BLOCK
        last = first + QUERY_BLOCK
        key = lax.broadcasted_iota(jnp.int32, (last, QUERY_BLOCK), 0)
        query = first + lax.broadcasted_iota(jnp.int32, (last, QUERY_BLOCK), 1)
        allowed = (key <= query) & (key >= start[:, first:last])
        bias[:last, first:last] = jnp.where(allowed, 0.0, MASKED)


def attend_kernel(
    row, own, other, own_row, other_row, own_weight, other_weight, inverse, cosine, sine, start,
    query_out, key_out, value_out, logs_out, mixed_out, pre, key_rows, bias, mixed,
):
    half = own.shape[0]
    group = 2 * half
    heads = query_out.shape[0] // HEAD_DIM
    first = pl.multiple_of(row[0] * half, 128)
    second = pl.multiple_of((1 - row[0]) * half, 128)
    scale = inverse[...]
    total = dot_t(own_weight[...], own[...]) + dot_t(other_weight[...], other[...])
    pre[:, pl.ds(first, half)] = total * scale[:, :half]
    total = dot_t(own_weight[...], own_row[...]) + dot_t(other_weight[...], other_row[...])
    pre[:, pl.ds(second, half)] = total * scale[:, half:]
    write_bias(bias, start)

    def turned(base):
        low = pre[pl.ds(base, HALF), :]
        high = pre[pl.ds(base + HALF, HALF), :]
        cos, sin = cosine[...], sine[...]
        return jnp.concatenate([low * cos - high * sin, high * cos + low * sin], axis=0)

    keys = turned(heads * HEAD_DIM).astype(BF)
    key_out[...] = keys
    key_rows[...] = keys.astype(F32).T.astype(BF)
    value_out[...] = pre[(heads + 1) * HEAD_DIM :, :].astype(BF)

    def head(index, carry):
        base = pl.multiple_of(index * HEAD_DIM, HEAD_DIM)
        place = pl.ds(base, HEAD_DIM)
        query_out[place, :] = (turned(base).astype(BF).astype(F32) * HEAD_DIM ** (-0.5)).astype(BF)
        for block in range(group // QUERY_BLOCK):
            low = block * QUERY_BLOCK
            high = low + QUERY_BLOCK
            scores = dot(key_rows[:high, :], query_out[place, low:high]) + bias[:high, low:high]
            peak = jnp.max(scores, axis=0, keepdims=True)
            weights = jnp.exp(scores - peak)
            totals = jnp.sum(weights, axis=0, keepdims=True)
            probs = (weights * (1.0 / totals)).astype(BF)
            mixed[place, low:high] = dot(value_out[:, :high], probs)
            logs_out[pl.ds(index, 1), low:high] = peak + jnp.log(totals)
        return carry

    lax.fori_loop(0, heads, head, 0)
    mixed_out[:, :half] = mixed[:, pl.ds(first, half)].astype(BF)
    mixed_out[:, half:] = mixed[:, pl.ds(second, half)].astype(BF)


def in_vmem(count):
    return [pl.BlockSpec(memory_space=pltpu.VMEM)] * count


def attend(
    row, own, other, own_row, other_row, own_weight, other_weight, inverse, cosine, sine, start
):
    group = 2 * own.shape[0]
    width = own_weight.shape[0]
    wide = width - 2 * HEAD_DIM
    heads = wide // HEAD_DIM
    cost = 4 * width * own.shape[1] * group + 3 * heads * group * group * HEAD_DIM
    return pl.pallas_call(
        attend_kernel,
        out_shape=(
            jax.ShapeDtypeStruct((wide, group), BF),
            jax.ShapeDtypeStruct((HEAD_DIM, group), BF),
            jax.ShapeDtypeStruct((HEAD_DIM, group), BF),
            jax.ShapeDtypeStruct((heads, group), F32),
            jax.ShapeDtypeStruct((wide, group), BF),
        ),
        in_specs=[pl.BlockSpec(memory_space=pltpu.SMEM)] + in_vmem(10),
        out_specs=tuple(in_vmem(5)),
        scratch_shapes=[
            pltpu.VMEM((width, group), F32),
            pltpu.VMEM((group, HEAD_DIM), BF),
            pltpu.VMEM((group, group), F32),
            pltpu.VMEM((wide, group), F32),
        ],
        compiler_params=pltpu.CompilerParams(vmem_limit_bytes=VMEM_BYTES),
        cost_estimate=pl.CostEstimate(
            flops=2 * cost, bytes_accessed=10**7, transcendentals=heads * group * group
        ),
        name="attend",
    )(
        row, own, other, own_row, other_row, own_weight, other_weight, inverse, cosine, sine, start
    )


def attend_back_kernel(
    row, query, key, value, logs, grad, grad_row, inverse, cosine, sine, start,
    grad_out, key_rows, value_rows, bias, grads, grad_query, grad_key, grad_value,
):
    group = query.shape[1]
    half = group // 2
    heads = query.shape[0] // HEAD_DIM
    first = pl.multiple_of(row[0] * half, 128)
    second = pl.multiple_of((1 - row[0]) * half, 128)
    grads[:, pl.ds(first, half)] = grad[...]
    grads[:, pl.ds(second, half)] = grad_row[...]
    write_bias(bias, start)
    key_rows[...] = key[...].astype(F32).T.astype(BF)
    value_rows[...] = value[...].astype(F32).T.astype(BF)
    grad_key[...] = jnp.zeros_like(grad_key)
    grad_value[...] = jnp.zeros_like(grad_value)
    cos, sin = cosine[...], sine[...]

    def turned_back(full):
        low, high = full[:HALF], full[HALF:]
        return jnp.concatenate([low * cos + high * sin, high * cos - low * sin], axis=0)

    def head(index, carry):
        place = pl.ds(pl.multiple_of(index * HEAD_DIM, HEAD_DIM), HEAD_DIM)
        for block in range(group // QUERY_BLOCK):
            low = block * QUERY_BLOCK
            high = low + QUERY_BLOCK
            queries = query[place, low:high]
            outs = grads[place, low:high]
            scores = dot(key_rows[:high, :], queries) + bias[:high, low:high]
            probs = jnp.exp(scores - logs[pl.ds(index, 1), low:high])
            grad_probs = probs * dot(value_rows[:high, :], outs)
            total = jnp.sum(grad_probs, axis=0, keepdims=True)
            grad_scores = (grad_probs - probs * total).astype(BF)
            grad_query[place, low:high] = dot(key[:, :high], grad_scores) * HEAD_DIM ** (-0.5)
            grad_key[:high, :] += dot_t(grad_scores, queries)
            grad_value[:high, :] += dot_t(probs.astype(BF), outs)
        grad_query[place, :] = turned_back(grad_query[place, :])
        return carry

    lax.fori_loop(0, heads, head, 0)
    wide = heads * HEAD_DIM
    grad_query[wide : wide + HEAD_DIM, :] = turned_back(grad_key[...].T)
    grad_query[wide + HEAD_DIM :, :] = grad_value[...].T
    scale = inverse[...]
    grad_out[:, :half] = (grad_query[:, pl.ds(first, half)] * scale[:, :half]).astype(BF)
    grad_out[:, half:] = (grad_query[:, pl.ds(second, half)] * scale[:, half:]).astype(BF)


def attend_back(row, query, key, value, logs, grad, grad_row, inverse, cosine, sine, start):
    wide, group = query.shape
    heads = wide // HEAD_DIM
    width = wide + 2 * HEAD_DIM
    cost = 10 * heads * group * group * HEAD_DIM
    return pl.pallas_call(
        attend_back_kernel,
        out_shape=jax.ShapeDtypeStruct((width, group), BF),
        in_specs=[pl.BlockSpec(memory_space=pltpu.SMEM)] + in_vmem(10),
        out_specs=in_vmem(1)[0],
        scratch_shapes=[
            pltpu.VMEM((group, HEAD_DIM), BF),
            pltpu.VMEM((group, HEAD_DIM), BF),
            pltpu.VMEM((group, group), F32),
            pltpu.VMEM((wide, group), BF),
            pltpu.VMEM((width, group), F32),
            pltpu.VMEM((group, HEAD_DIM), F32),
            pltpu.VMEM((group, HEAD_DIM), F32),
        ],
        compiler_params=pltpu.CompilerParams(vmem_limit_bytes=VMEM_BYTES),
        cost_estimate=pl.CostEstimate(
            flops=4 * cost, bytes_accessed=5 * 10**6, transcendentals=heads * group * group
        ),
        name="attend_back",
    )(row, query, key, value, logs, grad, grad_row, inverse, cosine, sine, start)


def prepare_kernel(col, query, key, value, own, other, turned):
    wide = query.shape[1] // 2
    mine = pl.multiple_of(col[0] * wide, 128)
    theirs = pl.multiple_of((1 - col[0]) * wide, 128)
    own[:wide, :] = query[:, pl.ds(mine, wide)].T
    other[:wide, :] = query[:, pl.ds(theirs, wide)].T
    mine = pl.multiple_of(col[0] * HEAD_DIM, HEAD_DIM)
    theirs = pl.multiple_of((1 - col[0]) * HEAD_DIM, HEAD_DIM)
    for index, source in enumerate((key, value)):
        turned[...] = source[...].T
        place = slice(wide + index * HEAD_DIM, wide + (index + 1) * HEAD_DIM)
        own[place, :] = turned[pl.ds(mine, HEAD_DIM), :]
        other[place, :] = turned[pl.ds(theirs, HEAD_DIM), :]


def prepare(col, query, key, value):
    depth = query.shape[0]
    shape = jax.ShapeDtypeStruct((query.shape[1] // 2 + 2 * HEAD_DIM, depth), BF)
    return pl.pallas_call(
        prepare_kernel,
        out_shape=(shape, shape),
        in_specs=[pl.BlockSpec(memory_space=pltpu.SMEM)] + in_vmem(3),
        out_specs=tuple(in_vmem(2)),
        scratch_shapes=[pltpu.VMEM((2 * HEAD_DIM, depth), BF)],
        compiler_params=pltpu.CompilerParams(vmem_limit_bytes=VMEM_BYTES),
        cost_estimate=pl.CostEstimate(flops=0, bytes_accessed=10**7, transcendentals=0),
        name="prepare",
    )(col, query, key, value)


def interleave_kernel(col, first, second, own, other):
    half = first.shape[1] // 2
    for tile in range(half // 128):
        low = tile * 128
        for out, index in ((own, col[0]), (other, 1 - col[0])):
            place = pl.ds(pl.multiple_of(index * half + low, 128), 128)
            out[:, 2 * low : 2 * low + 128] = first[:, place]
            out[:, 2 * low + 128 : 2 * low + 256] = second[:, place]


def interleave(col, first, second):
    depth, whole = first.shape
    rows = 128
    spec = pl.BlockSpec((rows, whole), lambda step, place: (step, 0))
    shape = jax.ShapeDtypeStruct((depth, whole), first.dtype)
    return pl.pallas_call(
        interleave_kernel,
        out_shape=(shape, shape),
        grid_spec=pltpu.PrefetchScalarGridSpec(
            num_scalar_prefetch=1,
            grid=(depth // rows,),
            in_specs=[spec, spec],
            out_specs=(spec, spec),
        ),
        compiler_params=pltpu.CompilerParams(vmem_limit_bytes=VMEM_BYTES),
        cost_estimate=pl.CostEstimate(
            flops=0, bytes_accessed=8 * depth * whole, transcendentals=0
        ),
        name="interleave",
    )(col, first, second)


def ffn_kernel(own, other, own_weight, other_weight, grad, inverse, hidden_out, grad_out):
    rows = own.shape[0] // 3
    for block in range(3):
        place = slice(block * rows, (block + 1) * rows)
        both = dot(own[place, :], own_weight[...]) + dot(other[place, :], other_weight[...])
        scale = inverse[place, :]
        both = both * scale
        gate, up = both[:, :128], both[:, 128:]
        sigmoid = 1.0 / (1.0 + jnp.exp(-gate))
        active = gate * sigmoid
        hidden_out[place, :] = (active * up).astype(BF)
        back = grad[place, :].astype(F32) * scale
        grad_out[place, :128] = (back * up * sigmoid * (1.0 + gate * (1.0 - sigmoid))).astype(BF)
        grad_out[place, 128:] = (back * active).astype(BF)


def ffn(own, other, own_weight, other_weight, grad, inverse):
    group, depth = own.shape
    wide = own_weight.shape[1]
    tiles = wide // 256
    return pl.pallas_call(
        ffn_kernel,
        out_shape=(
            jax.ShapeDtypeStruct((group, wide // 2), BF),
            jax.ShapeDtypeStruct((group, wide), BF),
        ),
        grid=(tiles,),
        in_specs=[
            pl.BlockSpec((group, depth), lambda step: (0, 0)),
            pl.BlockSpec((group, depth), lambda step: (0, 0)),
            pl.BlockSpec((depth, 256), lambda step: (0, step)),
            pl.BlockSpec((depth, 256), lambda step: (0, step)),
            pl.BlockSpec((group, 128), lambda step: (0, step)),
            pl.BlockSpec((group, 1), lambda step: (0, 0)),
        ],
        out_specs=(
            pl.BlockSpec((group, 128), lambda step: (0, step)),
            pl.BlockSpec((group, 256), lambda step: (0, step)),
        ),
        compiler_params=pltpu.CompilerParams(vmem_limit_bytes=VMEM_BYTES),
        cost_estimate=pl.CostEstimate(
            flops=4 * group * depth * wide,
            bytes_accessed=4 * depth * wide + 10 * group * wide,
            transcendentals=group * wide,
        ),
        name="ffn",
    )(own, other, own_weight, other_weight, grad, inverse)


def grads_kernel(pair, own, row, grad, grad_row, keep, send, turned, left):
    depth = own.shape[1]
    half = own.shape[0]
    rows = depth // 2
    lines = keep.shape[0]
    size = rows // lines

    @pl.when(pl.program_id(0) == 0)
    def _():
        turned[:, :half] = own[...].T
        turned[:, half:] = row[...].T
        for line in range(lines):
            for base, index in ((0, pair[0]), (rows, 1 - pair[0])):
                place = pl.ds(pl.multiple_of((2 * line + index) * size, size), size)
                left[base + line * size : base + (line + 1) * size, :] = turned[place, :]

    right = jnp.concatenate([grad[...], grad_row[...]], axis=0)
    keep[...] = dot(left[:rows, :], right).astype(BF).reshape(keep.shape)
    send[...] = dot(left[rows:, :], right).astype(BF).reshape(send.shape)


def grads(pair, lines, own, row, grad, grad_row):
    half, depth = own.shape
    wide = grad.shape[1]
    size = depth // (2 * lines)
    shape = jax.ShapeDtypeStruct((lines, size, wide), BF)
    out = pl.BlockSpec((lines, size, 256), lambda step: (0, 0, step))
    return pl.pallas_call(
        grads_kernel,
        out_shape=(shape, shape),
        grid=(wide // 256,),
        in_specs=[
            pl.BlockSpec(memory_space=pltpu.SMEM),
            pl.BlockSpec((half, depth), lambda step: (0, 0)),
            pl.BlockSpec((half, depth), lambda step: (0, 0)),
            pl.BlockSpec((half, 256), lambda step: (0, step)),
            pl.BlockSpec((half, 256), lambda step: (0, step)),
        ],
        out_specs=(out, out),
        scratch_shapes=[
            pltpu.VMEM((depth, 2 * half), BF),
            pltpu.VMEM((depth, 2 * half), BF),
        ],
        compiler_params=pltpu.CompilerParams(vmem_limit_bytes=VMEM_BYTES),
        cost_estimate=pl.CostEstimate(
            flops=4 * half * depth * wide,
            bytes_accessed=4 * half * (depth + wide) + 2 * depth * wide,
            transcendentals=0,
        ),
        name="grads",
    )(pair, own, row, grad, grad_row)


def assemble_kernel(col, own, moved, first, second):
    half = first.shape[1] // 2
    for tile in range(half // 128):
        low = tile * 128
        for source, index in ((own, col[0]), (moved, 1 - col[0])):
            place = pl.ds(pl.multiple_of(index * half + low, 128), 128)
            first[:, place] = source[:, 2 * low : 2 * low + 128].astype(F32)
            second[:, place] = source[:, 2 * low + 128 : 2 * low + 256].astype(F32)


def assemble(col, own, moved):
    shape = jax.ShapeDtypeStruct(own.shape, F32)
    return pl.pallas_call(
        assemble_kernel,
        out_shape=(shape, shape),
        in_specs=[pl.BlockSpec(memory_space=pltpu.SMEM)] + in_vmem(2),
        out_specs=tuple(in_vmem(2)),
        cost_estimate=pl.CostEstimate(flops=0, bytes_accessed=14 * own.size, transcendentals=0),
        name="assemble",
    )(col, own, moved)


def total(*terms):
    result = terms[0].astype(F32)
    for term in terms[1:]:
        result = result + term.astype(F32)
    return result


def pair_swap(value):
    return lax.ppermute(value, "dp", [(i, i ^ 1) for i in range(lax.axis_size("dp"))])


def line_reduce(piece):
    lines = lax.axis_size("dp") // 2
    place = lax.axis_index("dp") // 2
    right = left = ()
    for step in range(1, lines):
        going_right = piece(jnp.clip(lines - step + place, 0, lines - 1)) + right
        going_left = piece(jnp.clip(step + place - lines, 0, lines - 1)) + left
        sources = [(z, x) for z in range(min(step, lines - 1)) for x in range(2)]
        last = lines - 1
        right = (
            lax.ppermute(
                total(*going_right).astype(BF),
                "dp",
                [(2 * z + x, 2 * z + 2 + x) for z, x in sources],
            ),
        )
        left = (
            lax.ppermute(
                total(*going_left).astype(BF),
                "dp",
                [(2 * (last - z) + x, 2 * (last - z) - 2 + x) for z, x in sources],
            ),
        )
    return total(*(piece(place) + right + left))


def take(value, index, axis=0):
    return lax.dynamic_index_in_dim(value, index, axis, keepdims=False)


def own_first(lines, col):
    half = lines // 2
    return lambda z: ((z // half) ^ col) * half + z % half


def plain(z):
    return z


def cut(block):
    size = lax.axis_size("dp")
    pair = lax.axis_index("dp") % 2
    parts = block.reshape(size // 2, 2, block.shape[0] // size, block.shape[1])
    return (take(parts, pair, 1), take(parts, 1 - pair, 1))


def pairs_then_line(keep, send, place):
    moved = pair_swap(send)
    return line_reduce(lambda z: (take(keep, place(z)), take(moved, place(z))))


def line_then_pairs(block, place):
    size = lax.axis_size("dp")
    pair = lax.axis_index("dp") % 2
    parts = block.reshape(size // 2, 2, block.shape[0] // size, block.shape[1])
    sums = line_reduce(lambda z: (take(parts, place(z)),))
    return total(take(sums, pair), pair_swap(take(sums, 1 - pair).astype(BF)))


def everyone(value):
    value = value + swap(value, "row")
    size = lax.axis_size("dp")
    bit = 1
    while bit < size:
        value = value + lax.ppermute(value, "dp", [(i, i ^ bit) for i in range(size)])
        bit *= 2
    return value


def after(value, *earlier):
    return lax.optimization_barrier((value, *earlier))[0]


def shards(
    tokens,
    seq_lengths,
    attn_gain,
    q_weight,
    k_weight,
    v_weight,
    o_weight,
    ffn_gain,
    gate_weight,
    up_weight,
    down_weight,
    out_grad,
):
    row = lax.axis_index("row")
    col = lax.axis_index("col")
    rows = tokens.shape[0]
    group = 2 * rows
    q_half = q_weight.shape[1] // 2
    k_half = k_weight.shape[1] // 2
    f_half = gate_weight.shape[1] // 2
    lines = lax.axis_size("dp") // 2

    def part(value, index, size, axis):
        return lax.dynamic_slice_in_dim(value, index * size, size, axis)

    tokens_row = swap(tokens, "row")
    scaled_own = (tokens.astype(F32) * attn_gain).astype(BF)
    scaled_own_other = swap(scaled_own, "col")
    qkv_own, qkv_other = prepare(col[None], q_weight, k_weight, v_weight)
    qkv_recv = swap(qkv_other, "col")
    wide_own, wide_other = interleave(col[None], gate_weight, up_weight)
    wide_recv = swap(wide_other, "col")
    down_own = part(down_weight, col, f_half, 0)
    down_other = part(down_weight, 1 - col, f_half, 0)
    down_recv = swap(down_other, "col")

    places = jnp.arange(group, dtype=jnp.int32)
    start = layout(seq_lengths[0], places)
    cosine, sine = rotary_tables(places - start)
    start = start[None, :]
    which = row[None]

    grad_row = swap(after(out_grad, tokens_row), "row")
    own = tokens.astype(F32)
    away = tokens_row.astype(F32)
    scaled_row = (away * attn_gain).astype(BF)
    scaled_row_other = swap(scaled_row, "col")
    squares = jnp.concatenate([jnp.sum(own * own, axis=1), jnp.sum(away * away, axis=1)])
    squares = squares + swap(squares, "col")
    inverse_one = lax.rsqrt(squares / D + EPSILON)
    query, keys, values, logs, mixed = attend(
        which,
        scaled_own,
        scaled_own_other,
        scaled_row,
        scaled_row_other,
        qkv_own,
        qkv_recv,
        inverse_one[None, :],
        cosine,
        sine,
        start,
    )
    mixed_other = swap(mixed, "col")
    o_own = part(o_weight, col, q_half, 0)
    o_other = part(o_weight, 1 - col, q_half, 0)
    partial = outer(mixed, o_own) + outer(mixed_other, o_other)
    sent = partial.astype(BF)
    moved_own = swap(sent[rows:], "row")
    moved_row = swap(sent[:rows], "row")

    out_other = swap(out_grad, "col")
    grad_row_other = swap(grad_row, "col")
    hidden_grad = (dot_t(out_grad, down_own) + dot_t(out_other, down_recv)).astype(BF)
    hidden_grad_row = (dot_t(grad_row, down_own) + dot_t(grad_row_other, down_recv)).astype(BF)

    def feed(base, mine, moved, grad):
        stream = base + mine + moved.astype(F32)
        scaled = (stream * ffn_gain).astype(BF)
        squares = jnp.sum(stream * stream, axis=1)
        squares = squares + swap(squares, "col")
        inverse = lax.rsqrt(squares / D + EPSILON)
        scaled_other = swap(scaled, "col")
        hidden, wide = ffn(scaled, scaled_other, wide_own, wide_recv, grad, inverse[:, None])
        return (stream, inverse, scaled, scaled_other, hidden, wide)

    def feed_back(wide):
        moved = swap(dot_t(wide, wide_recv).astype(BF), "col")
        back = dot_t(wide, wide_own) + moved.astype(F32)
        return (back, swap(back.astype(BF), "row"))

    stream, inverse, scaled, scaled_other, hidden, wide = feed(
        own, partial[:rows], moved_own, hidden_grad
    )
    back, back_row_moved = feed_back(wide)
    stream_row, inverse_row, scaled_row_two, scaled_row_two_other, hidden_row, wide_row = feed(
        away, partial[rows:], moved_row, hidden_grad_row
    )
    hidden_other = swap(hidden, "col")
    hidden_row_other = swap(hidden_row, "col")

    pair = lax.axis_index("dp") % 2
    hidden_both = jnp.concatenate(
        [
            jnp.concatenate([hidden, hidden_other], axis=1),
            jnp.concatenate([hidden_row, hidden_row_other], axis=1),
        ],
        axis=0,
    )
    grad_two = jnp.concatenate([out_grad, grad_row], axis=0)
    columns = grad_two.shape[1] // 2
    mirrored = own_first(lines, col)
    down_first = outer(hidden_both, grad_two[:, :columns]).astype(BF)
    down_sum_first = line_then_pairs(down_first, mirrored)
    wide_keep, wide_send = grads(pair[None], lines, scaled, scaled_row_two, wide, wide_row)
    wide_sum = pairs_then_line(wide_keep, wide_send, plain)
    back_row, back_moved = feed_back(wide_row)
    down_second = outer(hidden_both, grad_two[:, columns:]).astype(BF)
    down_sum_second = pairs_then_line(*cut(down_second), mirrored)
    wide_keep_other, wide_send_other = grads(
        pair[None], lines, scaled_other, scaled_row_two_other, wide, wide_row
    )
    wide_sum_other = pairs_then_line(wide_keep_other, wide_send_other, plain)
    gate_sum, up_sum = assemble(col[None], wide_sum, swap(wide_sum_other.astype(BF), "col"))
    down_sum = jnp.concatenate([down_sum_first, down_sum_second], axis=1)

    result_sent = dot(hidden_row, down_own) + dot(hidden_row_other, down_other)
    result_moved = swap(result_sent.astype(BF), "row")
    result = total(
        stream, dot(hidden, down_own) + dot(hidden_other, down_other), result_moved
    ).astype(BF)

    def norm_back(base, back, moved, stream, inverse):
        back = back + moved.astype(F32)
        scaled = back * ffn_gain
        inner = jnp.sum(scaled * stream, axis=1)
        inner = inner + swap(inner, "col")
        grad = base.astype(F32) + scaled - stream * (inverse**2 * inner / D)[:, None]
        return (back, grad, grad.astype(BF))

    def mix_back(branch):
        moved = swap(dot_t(o_other, branch).astype(BF), "col")
        return total(dot_t(o_own, branch), moved).astype(BF)

    back_row, grad_one_row, branch_row = norm_back(
        grad_row, back_row, back_row_moved, stream_row, inverse_row
    )
    mixed_grad_row = mix_back(branch_row)
    back, grad_one, branch = norm_back(out_grad, back, back_moved, stream, inverse)
    mixed_grad = mix_back(branch)
    gain_two = jnp.sum(back * stream, axis=0)
    mixed_both = jnp.concatenate([mixed, mixed_other], axis=0)
    o_grad = dot(mixed_both, jnp.concatenate([branch, branch_row], axis=0)).astype(BF)
    o_sum = pairs_then_line(*cut(o_grad), mirrored)

    grad_qkv = attend_back(
        which,
        query,
        keys,
        values,
        logs,
        mixed_grad,
        mixed_grad_row,
        inverse_one[None, :],
        cosine,
        sine,
        start,
    )
    grad_qkv_both = jnp.concatenate([grad_qkv, swap(grad_qkv, "col")], axis=0)
    scaled_one = jnp.concatenate([scaled_own, scaled_row], axis=0)
    qkv_grad = lax.dot_general(
        scaled_one, grad_qkv_both, (((0,), (1,)), ((), ())), preferred_element_type=F32
    ).astype(BF)
    qkv_sum = pairs_then_line(*cut(qkv_grad), plain)
    last = outer(grad_qkv_both, jnp.concatenate([qkv_own, qkv_other], axis=0))
    last_moved = swap(last[rows:].astype(BF), "row")
    gain_one = jnp.sum(last[:rows] * own, axis=0) + jnp.sum(last[rows:] * away, axis=0)
    gains = everyone(jnp.stack([gain_one, gain_two]))
    last = last[:rows] + last_moved.astype(F32)
    scaled_last = last * attn_gain
    inner_one = jnp.sum(scaled_last * own, axis=1)
    inner_one = inner_one + swap(inner_one, "col")
    grad_tokens = (
        grad_one
        + scaled_last
        - own * (inverse_one[:rows] ** 2 * inner_one / D)[:, None]
    ).astype(BF)
    width = q_half + 2 * k_half

    def pick(first, size):
        return ordered(
            qkv_sum[:, first : first + size],
            qkv_sum[:, width + first : width + first + size],
            col,
            1,
        )

    return (
        result,
        grad_tokens,
        gains[0],
        pick(0, q_half),
        pick(q_half, k_half),
        pick(q_half + k_half, k_half),
        o_sum,
        gains[1],
        gate_sum,
        up_sum,
        down_sum,
    )


def solution(mesh):
    placed = (
        P(("dp", "row"), "col"),
        P("dp", None),
        P("col"),
        P("col", "row"),
        P("col", "row"),
        P("col", "row"),
        P("row", "col"),
        P("col"),
        P("col", "row"),
        P("col", "row"),
        P("row", "col"),
        P(("dp", "row"), "col"),
    )
    return jax.shard_map(
        shards,
        mesh=mesh,
        in_specs=placed,
        out_specs=(
            P(("dp", "row"), "col"),
            P(("dp", "row"), "col"),
            P("col"),
            P(("col", "dp"), "row"),
            P(("col", "dp"), "row"),
            P(("col", "dp"), "row"),
            P(("row", "dp"), "col"),
            P("col"),
            P(("col", "dp"), "row"),
            P(("col", "dp"), "row"),
            P(("row", "dp"), "col"),
        ),
        check_vma=False,
    )
```

```python
import functools

import jax
import jax.numpy as jnp
from jax import lax
from jax.experimental import pallas as pl
from jax.experimental.pallas import tpu as pltpu
from jax.sharding import PartitionSpec as P

D = 2048
HEAD_DIM = 64

EPSILON = 1e-05
MASKED = -1e30
BF = jnp.bfloat16
F32 = jnp.float32


def dot(left, right):
    return jnp.dot(left, right, preferred_element_type=F32)


def dot_t(left, right):
    return lax.dot_general(left, right, (((1,), (1,)), ((), ())), preferred_element_type=F32)


def outer(left, right):
    return lax.dot_general(left, right, (((0,), (0,)), ((), ())), preferred_element_type=F32)


def swap(value, axis):
    return lax.ppermute(value, axis, [(0, 1), (1, 0)])


def ordered(own, other, index, axis):
    return jnp.where(
        index == 0,
        jnp.concatenate([own, other], axis=axis),
        jnp.concatenate([other, own], axis=axis),
    )


def layout(lengths, places):
    ends = jnp.cumsum(lengths)
    starts = ends - lengths
    segment = jnp.sum((places[:, None] >= ends[None, :]).astype(jnp.int32), axis=1)
    picked = (segment[:, None] == jnp.arange(lengths.shape[0], dtype=jnp.int32)[None, :]).astype(
        jnp.int32
    )
    return jnp.sum(picked * starts[None, :], axis=1)


def rotary_tables(position):
    half_dim = HEAD_DIM // 2
    freq = 10000.0 ** (-2.0 * jnp.arange(half_dim, dtype=F32) / HEAD_DIM)
    angle = freq[:, None] * position.astype(F32)[None, :]
    return (jnp.cos(angle), jnp.sin(angle))


QUERY_BLOCK = 256
HALF = HEAD_DIM // 2
VMEM_BYTES = 36 * 1024 * 1024
SMALL = pl.CostEstimate(flops=10**6, bytes_accessed=10**5, transcendentals=0)


def write_bias(bias, start):
    group = bias.shape[0]
    for block in range(group // QUERY_BLOCK):
        first = block * QUERY_BLOCK
        last = first + QUERY_BLOCK
        key = lax.broadcasted_iota(jnp.int32, (last, QUERY_BLOCK), 0)
        query = first + lax.broadcasted_iota(jnp.int32, (last, QUERY_BLOCK), 1)
        allowed = (key <= query) & (key >= start[:, first:last])
        bias[:last, first:last] = jnp.where(allowed, 0.0, MASKED)


def attend_kernel(
    row, own, other, own_row, other_row, own_weight, other_weight, inverse, cosine, sine, start,
    query_out, key_out, value_out, logs_out, mixed_out, pre, key_rows, bias, mixed,
):
    half = own.shape[0]
    group = 2 * half
    heads = query_out.shape[0] // HEAD_DIM
    first = pl.multiple_of(row[0] * half, 128)
    second = pl.multiple_of((1 - row[0]) * half, 128)
    scale = inverse[...]
    total = dot_t(own_weight[...], own[...]) + dot_t(other_weight[...], other[...])
    pre[:, pl.ds(first, half)] = total * scale[:, :half]
    total = dot_t(own_weight[...], own_row[...]) + dot_t(other_weight[...], other_row[...])
    pre[:, pl.ds(second, half)] = total * scale[:, half:]
    write_bias(bias, start)

    def turned(base):
        low = pre[pl.ds(base, HALF), :]
        high = pre[pl.ds(base + HALF, HALF), :]
        cos, sin = cosine[...], sine[...]
        return jnp.concatenate([low * cos - high * sin, high * cos + low * sin], axis=0)

    keys = turned(heads * HEAD_DIM).astype(BF)
    key_out[...] = keys
    key_rows[...] = keys.astype(F32).T.astype(BF)
    value_out[...] = pre[(heads + 1) * HEAD_DIM :, :].astype(BF)

    def head(index, carry):
        base = pl.multiple_of(index * HEAD_DIM, HEAD_DIM)
        place = pl.ds(base, HEAD_DIM)
        query_out[place, :] = (turned(base).astype(BF).astype(F32) * HEAD_DIM ** (-0.5)).astype(BF)
        for block in range(group // QUERY_BLOCK):
            low = block * QUERY_BLOCK
            high = low + QUERY_BLOCK
            scores = dot(key_rows[:high, :], query_out[place, low:high]) + bias[:high, low:high]
            peak = jnp.max(scores, axis=0, keepdims=True)
            weights = jnp.exp(scores - peak)
            totals = jnp.sum(weights, axis=0, keepdims=True)
            probs = (weights * (1.0 / totals)).astype(BF)
            mixed[place, low:high] = dot(value_out[:, :high], probs)
            logs_out[pl.ds(index, 1), low:high] = peak + jnp.log(totals)
        return carry

    lax.fori_loop(0, heads, head, 0)
    mixed_out[:, :half] = mixed[:, pl.ds(first, half)].astype(BF)
    mixed_out[:, half:] = mixed[:, pl.ds(second, half)].astype(BF)


def in_vmem(count):
    return [pl.BlockSpec(memory_space=pltpu.VMEM)] * count


def attend(
    row, own, other, own_row, other_row, own_weight, other_weight, inverse, cosine, sine, start
):
    group = 2 * own.shape[0]
    width = own_weight.shape[0]
    wide = width - 2 * HEAD_DIM
    heads = wide // HEAD_DIM
    cost = 4 * width * own.shape[1] * group + 3 * heads * group * group * HEAD_DIM
    return pl.pallas_call(
        attend_kernel,
        out_shape=(
            jax.ShapeDtypeStruct((wide, group), BF),
            jax.ShapeDtypeStruct((HEAD_DIM, group), BF),
            jax.ShapeDtypeStruct((HEAD_DIM, group), BF),
            jax.ShapeDtypeStruct((heads, group), F32),
            jax.ShapeDtypeStruct((wide, group), BF),
        ),
        in_specs=[pl.BlockSpec(memory_space=pltpu.SMEM)] + in_vmem(10),
        out_specs=tuple(in_vmem(5)),
        scratch_shapes=[
            pltpu.VMEM((width, group), F32),
            pltpu.VMEM((group, HEAD_DIM), BF),
            pltpu.VMEM((group, group), F32),
            pltpu.VMEM((wide, group), F32),
        ],
        compiler_params=pltpu.CompilerParams(vmem_limit_bytes=VMEM_BYTES),
        cost_estimate=pl.CostEstimate(
            flops=2 * cost, bytes_accessed=10**7, transcendentals=heads * group * group
        ),
        name="attend",
    )(
        row, own, other, own_row, other_row, own_weight, other_weight, inverse, cosine, sine, start
    )


def attend_back_kernel(
    row, query, key, value, logs, grad, grad_row, inverse, cosine, sine, start,
    grad_out, key_rows, value_rows, bias, grads, grad_query, grad_key, grad_value,
):
    group = query.shape[1]
    half = group // 2
    heads = query.shape[0] // HEAD_DIM
    first = pl.multiple_of(row[0] * half, 128)
    second = pl.multiple_of((1 - row[0]) * half, 128)
    grads[:, pl.ds(first, half)] = grad[...]
    grads[:, pl.ds(second, half)] = grad_row[...]
    write_bias(bias, start)
    key_rows[...] = key[...].astype(F32).T.astype(BF)
    value_rows[...] = value[...].astype(F32).T.astype(BF)
    grad_key[...] = jnp.zeros_like(grad_key)
    grad_value[...] = jnp.zeros_like(grad_value)
    cos, sin = cosine[...], sine[...]

    def turned_back(full):
        low, high = full[:HALF], full[HALF:]
        return jnp.concatenate([low * cos + high * sin, high * cos - low * sin], axis=0)

    def head(index, carry):
        place = pl.ds(pl.multiple_of(index * HEAD_DIM, HEAD_DIM), HEAD_DIM)
        for block in range(group // QUERY_BLOCK):
            low = block * QUERY_BLOCK
            high = low + QUERY_BLOCK
            queries = query[place, low:high]
            outs = grads[place, low:high]
            scores = dot(key_rows[:high, :], queries) + bias[:high, low:high]
            probs = jnp.exp(scores - logs[pl.ds(index, 1), low:high])
            grad_probs = probs * dot(value_rows[:high, :], outs)
            total = jnp.sum(grad_probs, axis=0, keepdims=True)
            grad_scores = (grad_probs - probs * total).astype(BF)
            grad_query[place, low:high] = dot(key[:, :high], grad_scores) * HEAD_DIM ** (-0.5)
            grad_key[:high, :] += dot_t(grad_scores, queries)
            grad_value[:high, :] += dot_t(probs.astype(BF), outs)
        grad_query[place, :] = turned_back(grad_query[place, :])
        return carry

    lax.fori_loop(0, heads, head, 0)
    wide = heads * HEAD_DIM
    grad_query[wide : wide + HEAD_DIM, :] = turned_back(grad_key[...].T)
    grad_query[wide + HEAD_DIM :, :] = grad_value[...].T
    scale = inverse[...]
    grad_out[:, :half] = (grad_query[:, pl.ds(first, half)] * scale[:, :half]).astype(BF)
    grad_out[:, half:] = (grad_query[:, pl.ds(second, half)] * scale[:, half:]).astype(BF)


def attend_back(row, query, key, value, logs, grad, grad_row, inverse, cosine, sine, start):
    wide, group = query.shape
    heads = wide // HEAD_DIM
    width = wide + 2 * HEAD_DIM
    cost = 10 * heads * group * group * HEAD_DIM
    return pl.pallas_call(
        attend_back_kernel,
        out_shape=jax.ShapeDtypeStruct((width, group), BF),
        in_specs=[pl.BlockSpec(memory_space=pltpu.SMEM)] + in_vmem(10),
        out_specs=in_vmem(1)[0],
        scratch_shapes=[
            pltpu.VMEM((group, HEAD_DIM), BF),
            pltpu.VMEM((group, HEAD_DIM), BF),
            pltpu.VMEM((group, group), F32),
            pltpu.VMEM((wide, group), BF),
            pltpu.VMEM((width, group), F32),
            pltpu.VMEM((group, HEAD_DIM), F32),
            pltpu.VMEM((group, HEAD_DIM), F32),
        ],
        compiler_params=pltpu.CompilerParams(vmem_limit_bytes=VMEM_BYTES),
        cost_estimate=SMALL,
        name="attend_back",
    )(row, query, key, value, logs, grad, grad_row, inverse, cosine, sine, start)


def prepare_kernel(col, query, key, value, own, other, turned):
    wide = query.shape[1] // 2
    mine = pl.multiple_of(col[0] * wide, 128)
    theirs = pl.multiple_of((1 - col[0]) * wide, 128)
    own[:wide, :] = query[:, pl.ds(mine, wide)].T
    other[:wide, :] = query[:, pl.ds(theirs, wide)].T
    mine = pl.multiple_of(col[0] * HEAD_DIM, HEAD_DIM)
    theirs = pl.multiple_of((1 - col[0]) * HEAD_DIM, HEAD_DIM)
    for index, source in enumerate((key, value)):
        turned[...] = source[...].T
        place = slice(wide + index * HEAD_DIM, wide + (index + 1) * HEAD_DIM)
        own[place, :] = turned[pl.ds(mine, HEAD_DIM), :]
        other[place, :] = turned[pl.ds(theirs, HEAD_DIM), :]


def prepare(col, query, key, value):
    depth = query.shape[0]
    shape = jax.ShapeDtypeStruct((query.shape[1] // 2 + 2 * HEAD_DIM, depth), BF)
    return pl.pallas_call(
        prepare_kernel,
        out_shape=(shape, shape),
        in_specs=[pl.BlockSpec(memory_space=pltpu.SMEM)] + in_vmem(3),
        out_specs=tuple(in_vmem(2)),
        scratch_shapes=[pltpu.VMEM((2 * HEAD_DIM, depth), BF)],
        compiler_params=pltpu.CompilerParams(vmem_limit_bytes=VMEM_BYTES),
        cost_estimate=pl.CostEstimate(flops=0, bytes_accessed=10**7, transcendentals=0),
        name="prepare",
    )(col, query, key, value)


def interleave_kernel(col, first, second, own, other):
    for tile in range(own.shape[0]):
        for out, index in ((own, col[0]), (other, 1 - col[0])):
            place = pl.ds(pl.multiple_of((index * own.shape[0] + tile) * 128, 128), 128)
            out[tile, :, :128] = first[:, place]
            out[tile, :, 128:] = second[:, place]


def interleave(col, first, second):
    depth, whole = first.shape
    tiles = whole // 256
    rows = 128
    shape = jax.ShapeDtypeStruct((tiles, depth, 256), first.dtype)
    spec = pl.BlockSpec((rows, whole), lambda step, place: (step, 0))
    out = pl.BlockSpec((tiles, rows, 256), lambda step, place: (0, step, 0))
    return pl.pallas_call(
        interleave_kernel,
        out_shape=(shape, shape),
        grid_spec=pltpu.PrefetchScalarGridSpec(
            num_scalar_prefetch=1,
            grid=(depth // rows,),
            in_specs=[spec, spec],
            out_specs=(out, out),
        ),
        compiler_params=pltpu.CompilerParams(vmem_limit_bytes=VMEM_BYTES),
        cost_estimate=pl.CostEstimate(
            flops=0, bytes_accessed=8 * depth * whole, transcendentals=0
        ),
        name="interleave",
    )(col, first, second)


def hidden_kernel(*refs):
    ins, (weight, other_weight, out) = refs[:4], refs[4:]
    own, other = (
        (ins[0], ins[1]),
        (ins[2], ins[3]),
    )
    rows = own[0].shape[0]
    for index in range(2):
        product = dot_t(own[index][...], weight[...]) + dot_t(other[index][...], other_weight[...])
        out[index * rows : (index + 1) * rows, :] = product.astype(BF)


def hidden_product(own, row, other, row_other, weight, other_weight):
    rows = own.shape[0]
    return pl.pallas_call(
        hidden_kernel,
        out_shape=jax.ShapeDtypeStruct((2 * rows, weight.shape[0]), BF),
        in_specs=in_vmem(6),
        out_specs=in_vmem(1)[0],
        compiler_params=pltpu.CompilerParams(vmem_limit_bytes=VMEM_BYTES),
        cost_estimate=SMALL,
        name="hidden",
    )(own, row, other, row_other, weight, other_weight)


def ffn_kernel(own, other, other_next, own_weight, other_weight, grad, inverse, hidden_out, grad_out):
    scale = inverse[...]
    moved = jnp.concatenate([other[...], other_next[...]], axis=0)
    both = dot(own[...], own_weight[...]) + dot(moved, other_weight[...])
    both = both * scale
    gate, up = both[:, :128], both[:, 128:]
    sigmoid = 1.0 / (1.0 + jnp.exp(-gate))
    active = gate * sigmoid
    hidden_out[...] = (active * up).astype(BF)
    back = grad[...].astype(F32) * scale
    grad_out[:, :128] = (back * up * sigmoid * (1.0 + gate * (1.0 - sigmoid))).astype(BF)
    grad_out[:, 128:] = (back * active).astype(BF)


def ffn_next_kernel(hidden_in, grad_in, *refs):
    ffn_kernel(*refs)


def ffn(own, others, own_weight, other_weight, grad, inverse, before=None):
    rows, depth = own.shape
    tiles = own_weight.shape[0]
    wide = tiles * 256
    half = 0 if before is None else 1
    extra = [] if before is None else [pl.BlockSpec(memory_space=pl.ANY)] * 2
    return pl.pallas_call(
        ffn_kernel if before is None else ffn_next_kernel,
        out_shape=(
            jax.ShapeDtypeStruct((2 * rows, wide // 2), BF),
            jax.ShapeDtypeStruct((2 * rows, wide), BF),
        ),
        grid=(tiles,),
        in_specs=extra
        + [
            pl.BlockSpec((rows, depth), lambda step: (0, 0)),
            pl.BlockSpec((rows // 2, depth), lambda step: (0, 0)),
            pl.BlockSpec((rows // 2, depth), lambda step: (0, 0)),
            pl.BlockSpec((None, depth, 256), lambda step: (step, 0, 0)),
            pl.BlockSpec((None, depth, 256), lambda step: (step, 0, 0)),
            pl.BlockSpec((rows, 128), lambda step: (half, step)),
            pl.BlockSpec((rows, 1), lambda step: (0, 0)),
        ],
        out_specs=(
            pl.BlockSpec((rows, 128), lambda step: (half, step)),
            pl.BlockSpec((rows, 256), lambda step: (half, step)),
        ),
        input_output_aliases={} if before is None else {0: 0, 1: 1},
        compiler_params=pltpu.CompilerParams(vmem_limit_bytes=VMEM_BYTES),
        cost_estimate=SMALL,
        name="ffn",
    )(*(before or ()), own, *others, own_weight, other_weight, grad, inverse)


def grads_kernel(turn, flat, parts, inner, counts, place, *refs):
    lefts, rights = refs[: counts[0]], refs[counts[0] : counts[0] + counts[1]]
    keep, send, turned, left = refs[counts[0] + counts[1] :]
    depth = left.shape[0]
    rows = depth // 2

    def arrange(sources):
        low = 0
        for source in sources:
            if turn:
                turned[:, low : low + source.shape[0]] = source[...].T
                low += source.shape[0]
        full = turned if turn else sources[0]
        for index in range(rows // inner):
            for base, part in ((0, place[0]), (rows, 1 - place[0])):
                chosen = pl.ds(pl.multiple_of((2 * index + part) * inner, inner), inner)
                left[base + index * inner : base + (index + 1) * inner, :] = full[chosen, :]

    for part in range(parts):
        share = counts[0] // parts

        @pl.when(pl.program_id(0) == part)
        def _():
            arrange(lefts[part * share : (part + 1) * share])

    for base, out in ((rows, send), (0, keep)):
        low = 0
        for right in rights:
            if flat:
                product = dot_t(left[base : base + rows, :], right[...])
            else:
                product = dot(left[base : base + rows, :], right[...])
            out[:, low : low + product.shape[1]] = product.astype(BF)
            low += product.shape[1]


def grads(place, inner, lefts, rights, turn=True, flat=False, steps=1, parts=1):
    share = lefts[: len(lefts) // parts]
    depth = lefts[0].shape[1] if turn else lefts[0].shape[0]
    group = sum(one.shape[0] for one in share) if turn else lefts[0].shape[1]
    wide = sum(one.shape[0] if flat else one.shape[1] for one in rights)
    shape = jax.ShapeDtypeStruct((parts, depth // 2, wide), BF)
    if parts == 1:
        out = pl.BlockSpec((None, depth // 2, wide // steps), lambda step: (0, 0, step))
    else:
        out = pl.BlockSpec((None, depth // 2, wide), lambda step: (step, 0, 0))

    def whole(one):
        return pl.BlockSpec(one.shape, lambda step: (0, 0))

    def right_spec(one):
        if flat or steps == 1:
            return whole(one)
        return pl.BlockSpec((group, one.shape[1] // steps), lambda step: (0, step))

    return pl.pallas_call(
        functools.partial(grads_kernel, turn, flat, parts, inner, (len(lefts), len(rights))),
        out_shape=(shape, shape),
        grid=(max(steps, parts),),
        in_specs=[pl.BlockSpec(memory_space=pltpu.SMEM)]
        + [whole(one) for one in lefts]
        + [right_spec(one) for one in rights],
        out_specs=(out, out),
        scratch_shapes=[
            pltpu.VMEM((depth, group) if turn else (16, 128), BF),
            pltpu.VMEM((depth, group), BF),
        ],
        compiler_params=pltpu.CompilerParams(vmem_limit_bytes=VMEM_BYTES),
        cost_estimate=SMALL,
        name="grads",
    )(place, *lefts, *rights)


def tiles_in_row(weight):
    return jnp.concatenate([weight[tile] for tile in range(weight.shape[0])], axis=1)


def back_kernel(wide, weight, out, out_row):
    rows = out.shape[0]
    total = dot_t(wide[...], tiles_in_row(weight))
    out[...] = total[:rows].astype(BF)
    out_row[...] = total[rows:].astype(BF)


def back_next_kernel(wide, weight, moved, moved_row, out, out_row, sent, sent_row):
    rows = sent.shape[0]
    total = dot_t(wide[...], tiles_in_row(weight))
    for low, other, kept, going in ((0, moved, out, sent), (rows, moved_row, out_row, sent_row)):
        half = total[low : low + rows] + other[...].astype(F32)
        kept[...] = half
        going[...] = half.astype(BF)


def back_product(wide, weight, moved=()):
    group, depth = wide.shape
    tiles, rows, _ = weight.shape
    width = 256
    tile = pl.BlockSpec((group // 2, width), lambda step: (0, step))
    half = jax.ShapeDtypeStruct((group // 2, rows), BF)
    full = jax.ShapeDtypeStruct((group // 2, rows), F32)
    outs = (full, full, half, half) if moved else (half, half)
    return pl.pallas_call(
        back_next_kernel if moved else back_kernel,
        out_shape=outs,
        grid=(rows // width,),
        in_specs=[
            pl.BlockSpec((group, depth), lambda step: (0, 0)),
            pl.BlockSpec((tiles, width, 256), lambda step: (0, step, 0)),
        ]
        + [tile] * len(moved),
        out_specs=(tile,) * len(outs),
        compiler_params=pltpu.CompilerParams(vmem_limit_bytes=VMEM_BYTES),
        cost_estimate=SMALL,
        name="back",
    )(wide, weight, *moved)


def down_kernel(hidden, other, weight, other_weight, kept, sent):
    rows = kept.shape[0]
    total = dot(hidden[...], weight[...]) + dot(other[...], other_weight[...])
    kept[...] = total[:rows]
    sent[...] = total[rows:].astype(BF)


def down_product(hidden, other, weight, other_weight):
    group, depth = hidden.shape
    columns = weight.shape[1]
    width = 256
    tile = pl.BlockSpec((group // 2, width), lambda step: (0, step))
    whole = pl.BlockSpec((group, depth), lambda step: (0, 0))
    weights = pl.BlockSpec((depth, width), lambda step: (0, step))
    return pl.pallas_call(
        down_kernel,
        out_shape=(
            jax.ShapeDtypeStruct((group // 2, columns), F32),
            jax.ShapeDtypeStruct((group // 2, columns), BF),
        ),
        grid=(columns // width,),
        in_specs=[whole, whole, weights, weights],
        out_specs=(tile, tile),
        compiler_params=pltpu.CompilerParams(vmem_limit_bytes=VMEM_BYTES),
        cost_estimate=SMALL,
        name="down",
    )(hidden, other, weight, other_weight)


def last_kernel(grad, other, weight, other_weight, tokens, tokens_row, kept, sent, gain, turned, turned_other):
    rows = kept.shape[0]

    @pl.when(pl.program_id(0) == 0)
    def _():
        turned[...] = grad[...].T
        turned_other[...] = other[...].T

    total = dot(turned[...], weight[...]) + dot(turned_other[...], other_weight[...])
    kept[...] = total[:rows]
    sent[...] = total[rows:].astype(BF)
    gain[...] = jnp.sum(total[:rows] * tokens[...].astype(F32), axis=0, keepdims=True) + jnp.sum(
        total[rows:] * tokens_row[...].astype(F32), axis=0, keepdims=True
    )


def last_product(grad, other, weight, other_weight, tokens, tokens_row):
    depth, group = grad.shape
    columns = weight.shape[1]
    width = columns // 2
    tile = pl.BlockSpec((group // 2, width), lambda step: (0, step))
    whole = pl.BlockSpec((depth, group), lambda step: (0, 0))
    weights = pl.BlockSpec((depth, width), lambda step: (0, step))
    return pl.pallas_call(
        last_kernel,
        out_shape=(
            jax.ShapeDtypeStruct((group // 2, columns), F32),
            jax.ShapeDtypeStruct((group // 2, columns), BF),
            jax.ShapeDtypeStruct((1, columns), F32),
        ),
        grid=(2,),
        in_specs=[whole, whole, weights, weights, tile, tile],
        out_specs=(tile, tile, pl.BlockSpec((1, width), lambda step: (0, step))),
        scratch_shapes=[pltpu.VMEM((group, depth), BF), pltpu.VMEM((group, depth), BF)],
        compiler_params=pltpu.CompilerParams(vmem_limit_bytes=VMEM_BYTES),
        cost_estimate=SMALL,
        name="last",
    )(grad, other, weight, other_weight, tokens, tokens_row)


def assemble_kernel(col, own, moved, first, second):
    half = first.shape[1] // 2
    for tile in range(half // 128):
        low = tile * 128
        for source, index in ((own, col[0]), (moved, 1 - col[0])):
            place = pl.ds(pl.multiple_of(index * half + low, 128), 128)
            first[:, place] = source[:, 2 * low : 2 * low + 128].astype(F32)
            second[:, place] = source[:, 2 * low + 128 : 2 * low + 256].astype(F32)


def assemble(col, own, moved):
    shape = jax.ShapeDtypeStruct(own.shape, F32)
    return pl.pallas_call(
        assemble_kernel,
        out_shape=(shape, shape),
        in_specs=[pl.BlockSpec(memory_space=pltpu.SMEM)] + in_vmem(2),
        out_specs=tuple(in_vmem(2)),
        cost_estimate=pl.CostEstimate(flops=0, bytes_accessed=14 * own.size, transcendentals=0),
        name="assemble",
    )(col, own, moved)


def total(*terms):
    result = terms[0].astype(F32)
    for term in terms[1:]:
        result = result + term.astype(F32)
    return result


def take(value, index, axis=0):
    return lax.dynamic_index_in_dim(value, index, axis, keepdims=False)


def bits_of(size):
    return size.bit_length() - 1


def exchange(value, bit):
    size = lax.axis_size("dp")
    return lax.ppermute(value, "dp", [(i, i ^ (1 << bit)) for i in range(size)])


class Halving:
    def __init__(self, terms, left, flip):
        self.terms, self.left, self.flip = list(terms), list(left), flip

    def cut(self, bit):
        axis = self.left.index(bit)
        mine = (lax.axis_index("dp") >> bit) & 1
        if bit == bits_of(lax.axis_size("dp")) - 1:
            mine = mine ^ self.flip
        sent = total(*[take(term, 1 - mine, axis) for term in self.terms]).astype(BF)
        self.terms = [take(term, mine, axis) for term in self.terms]
        self.left.remove(bit)
        return sent

    def send(self, bit, sent):
        self.terms.append(exchange(sent, bit))

    def finish(self):
        return total(*self.terms)


def high_bits(skipped=()):
    return [b for b in reversed(range(bits_of(lax.axis_size("dp")))) if b not in skipped]


def everyone(value):
    value = value + swap(value, "row")
    size = lax.axis_size("dp")
    bit = 1
    while bit < size:
        value = value + lax.ppermute(value, "dp", [(i, i ^ bit) for i in range(size)])
        bit *= 2
    return value


def after(value, *earlier):
    return lax.optimization_barrier((value, *earlier))[0]


def shards(
    tokens,
    seq_lengths,
    attn_gain,
    q_weight,
    k_weight,
    v_weight,
    o_weight,
    ffn_gain,
    gate_weight,
    up_weight,
    down_weight,
    out_grad,
):
    row = lax.axis_index("row")
    col = lax.axis_index("col")
    rows = tokens.shape[0]
    group = 2 * rows
    q_half = q_weight.shape[1] // 2
    k_half = k_weight.shape[1] // 2
    f_half = gate_weight.shape[1] // 2
    lines = lax.axis_size("dp") // 2

    def part(value, index, size, axis):
        return lax.dynamic_slice_in_dim(value, index * size, size, axis)

    bits = bits_of(lax.axis_size("dp"))
    tokens_row = swap(tokens, "row")
    scaled_own = (tokens.astype(F32) * attn_gain).astype(BF)
    scaled_own_other = swap(scaled_own, "col")
    qkv_own, qkv_other = prepare(col[None], q_weight, k_weight, v_weight)
    qkv_recv = swap(qkv_other, "col")
    wide_own, wide_other = interleave(col[None], gate_weight, up_weight)
    wide_recv = swap(wide_other, "col")
    down_own = part(down_weight, col, f_half, 0)
    down_other = part(down_weight, 1 - col, f_half, 0)
    down_recv = swap(down_other, "col")

    places = jnp.arange(group, dtype=jnp.int32)
    start = layout(seq_lengths[0], places)
    cosine, sine = rotary_tables(places - start)
    start = start[None, :]
    which = row[None]

    tokens_row = after(tokens_row, wide_other)
    grad_row = swap(after(out_grad, tokens_row), "row")
    out_other = swap(out_grad, "col")
    own = tokens.astype(F32)
    away = tokens_row.astype(F32)
    scaled_row = (away * attn_gain).astype(BF)
    scaled_row_other = swap(scaled_row, "col")
    squares = jnp.concatenate([jnp.sum(own * own, axis=1), jnp.sum(away * away, axis=1)])
    squares = squares + swap(squares, "col")
    inverse_one = lax.rsqrt(squares / D + EPSILON)
    query, keys, values, logs, mixed = attend(
        after(which, down_other),
        scaled_own,
        scaled_own_other,
        scaled_row,
        scaled_row_other,
        qkv_own,
        qkv_recv,
        inverse_one[None, :],
        cosine,
        sine,
        start,
    )
    mixed_other = swap(mixed, "col")
    o_own = part(o_weight, col, q_half, 0)
    o_other = part(o_weight, 1 - col, q_half, 0)
    grad_row = after(grad_row, mixed)
    grad_row_other = swap(grad_row, "col")
    partial = outer(after(mixed, grad_row), o_own) + outer(mixed_other, o_other)
    sent_row = partial[rows:].astype(BF)
    sent_own = partial[:rows].astype(BF)
    moved_own = swap(sent_row, "row")
    moved_row = swap(sent_own, "row")

    hidden_grad = hidden_product(
        after(out_grad, sent_row, sent_own), grad_row, out_other, grad_row_other, down_own, down_recv
    )

    def feed(base, mine, moved, grad, before=None):
        stream = base + mine + moved.astype(F32)
        scaled = (stream * ffn_gain).astype(BF)
        squares = jnp.sum(stream * stream, axis=1)
        squares = squares + swap(squares, "col")
        inverse = lax.rsqrt(squares / D + EPSILON)
        scaled_other = (swap(scaled[: rows // 2], "col"), swap(scaled[rows // 2 :], "col"))
        outs = ffn(scaled, scaled_other, wide_own, wide_recv, grad, inverse[:, None], before)
        return (stream, inverse, scaled, scaled_other, outs)

    stream, inverse, scaled, scaled_other, first = feed(
        own, partial[:rows], after(moved_own, hidden_grad), hidden_grad
    )
    stream_row, inverse_row, scaled_row_two, scaled_row_two_other, second = feed(
        away, partial[rows:], after(moved_row, first[1]), hidden_grad, first
    )
    hidden, wide = second
    hidden_other = swap(hidden, "col")

    size = lax.axis_size("dp")

    def place_of(bit):
        return ((lax.axis_index("dp") >> bit) & 1)[None]

    def weight_grads(bit, flip, *args, parts=1, **options):
        lefts = args[0]
        turn = options.get("turn", True)
        depth = lefts[0].shape[1] if turn else lefts[0].shape[0]
        rows = depth * parts // size
        keep, send = grads(place_of(bit), rows << bit, *args, parts=parts, **options)
        left = high_bits((bit,))
        shape = (2,) * len(left) + (rows, keep.shape[-1])
        chunk = Halving([keep.reshape(shape)], left, flip)
        chunk.send(bit, send.reshape(shape))
        return (chunk, keep)

    def forward(chunk, bit, *earlier):
        chunk.terms[-1] = after(chunk.terms[-1], *earlier)
        sent = chunk.cut(bit)
        chunk.send(bit, sent)
        return sent

    wide_chunk, done = weight_grads(0, 0, [scaled, scaled_row_two], [wide], steps=2)
    back_first, back_first_row = back_product(after(wide, done), wide_recv)
    back_swapped = (swap(back_first, "col"), swap(back_first_row, "col"))
    done = back_first
    grad_two = after(jnp.concatenate([out_grad, grad_row], axis=0), hidden)
    down_chunk, done = weight_grads(
        1, col, [after(hidden, done), hidden_other], [grad_two], parts=2
    )

    back_part, back_part_row, back_sent_own, back_sent_row = back_product(
        after(wide, done), wide_own, back_swapped
    )
    back_row_moved = swap(back_sent_own, "row")
    back_moved = swap(back_sent_row, "row")

    def norm_back(base, back, moved, stream, inverse):
        back = back + moved.astype(F32)
        scaled = back * ffn_gain
        inner = jnp.sum(scaled * stream, axis=1)
        inner = inner + swap(inner, "col")
        grad = base.astype(F32) + scaled - stream * (inverse**2 * inner / D)[:, None]
        return (back, grad, grad.astype(BF))

    def mix_back(branch):
        moved = swap(dot_t(o_other, branch).astype(BF), "col")
        return total(dot_t(o_own, branch), moved).astype(BF)

    other_chunk, done = weight_grads(
        0, 0, [after(scaled_other[0], back_part), scaled_other[1], *scaled_row_two_other], [wide], steps=2
    )
    result_kept, result_sent = down_product(
        after(hidden, done), hidden_other, down_own, down_other
    )
    result_moved = swap(result_sent, "row")
    back_row, grad_one_row, branch_row = norm_back(
        grad_row, back_part_row, after(back_row_moved, result_kept), stream_row, inverse_row
    )
    wide_sent = forward(wide_chunk, 1, branch_row)
    mixed_grad_row = mix_back(after(branch_row, wide_sent))
    done = mixed_grad_row
    for bit in range(2, bits):
        done = forward(down_chunk, bit, done)
    back, grad_one, branch = norm_back(
        out_grad, back_part, after(back_moved, done), stream, inverse
    )
    mixed_grad = mix_back(branch)
    gain_two = jnp.sum(back * stream, axis=0)
    branches = jnp.concatenate([branch, branch_row], axis=0)
    o_chunk, done = weight_grads(1, col, [mixed, mixed_other], [branches], turn=False, parts=2)
    grad_qkv = attend_back(
        after(which, done),
        query,
        keys,
        values,
        logs,
        mixed_grad,
        mixed_grad_row,
        inverse_one[None, :],
        cosine,
        sine,
        start,
    )
    grad_qkv_other = swap(grad_qkv, "col")
    done = grad_qkv
    for bit in range(2, bits):
        done = forward(wide_chunk, bit, done)
    done = forward(other_chunk, 1, done)
    result = total(stream, result_kept, after(result_moved, done)).astype(BF)
    done = forward(o_chunk, 0, done)
    qkv_chunk, done = weight_grads(
        0, 0, [scaled_own, scaled_row], [after(grad_qkv, done), grad_qkv_other], flat=True
    )
    last, last_sent, gain_one = last_product(
        after(grad_qkv, done), grad_qkv_other, qkv_own, qkv_other, tokens, tokens_row
    )
    last_moved = swap(last_sent, "row")
    gains = jnp.concatenate([gain_one, gain_two[None, :]], axis=0)
    gains = gains + swap(gains, "row")

    gains_moved = exchange(gains, 0)
    done = forward(down_chunk, 0, gains)
    for bit in range(2, bits):
        done = forward(o_chunk, bit, done)
        done = forward(other_chunk, bit, done)
    last = last + after(last_moved, done).astype(F32)
    scaled_last = last * attn_gain
    inner_one = jnp.sum(scaled_last * own, axis=1)
    inner_one = inner_one + swap(inner_one, "col")
    grad_tokens = (
        grad_one
        + scaled_last
        - own * (inverse_one[:rows] ** 2 * inner_one / D)[:, None]
    ).astype(BF)
    done = forward(qkv_chunk, 1, done)

    def finish(chunk, *earlier):
        chunk.terms[-1] = after(chunk.terms[-1], *earlier)
        return chunk.finish()

    wide_sum = finish(wide_chunk, done)
    gains = gains + after(gains_moved, wide_sum)
    done = gains
    for bit in range(1, bits):
        gains_moved = exchange(gains, bit)
        if bit >= 2:
            done = forward(qkv_chunk, bit, done)
        gains = gains + after(gains_moved, done)
    down_sum = finish(down_chunk, done)
    o_sum = finish(o_chunk, down_sum)
    other_sum = finish(other_chunk, o_sum).astype(BF)
    gate_sum, up_sum = assemble(col[None], wide_sum, swap(other_sum, "col"))
    qkv_sum = finish(qkv_chunk, other_sum)
    width = q_half + 2 * k_half

    def pick(first, size):
        return ordered(
            qkv_sum[:, first : first + size],
            qkv_sum[:, width + first : width + first + size],
            col,
            1,
        )

    return (
        result,
        grad_tokens,
        gains[0],
        pick(0, q_half),
        pick(q_half, k_half),
        pick(q_half + k_half, k_half),
        o_sum,
        gains[1],
        gate_sum,
        up_sum,
        down_sum,
    )


def solution(mesh):
    placed = (
        P(("dp", "row"), "col"),
        P("dp", None),
        P("col"),
        P("col", "row"),
        P("col", "row"),
        P("col", "row"),
        P("row", "col"),
        P("col"),
        P("col", "row"),
        P("col", "row"),
        P("row", "col"),
        P(("dp", "row"), "col"),
    )
    return jax.shard_map(
        shards,
        mesh=mesh,
        in_specs=placed,
        out_specs=(
            P(("dp", "row"), "col"),
            P(("dp", "row"), "col"),
            P("col"),
            P(("col", "dp"), "row"),
            P(("col", "dp"), "row"),
            P(("col", "dp"), "row"),
            P(("row", "dp"), "col"),
            P("col"),
            P(("col", "dp"), "row"),
            P(("col", "dp"), "row"),
            P(("row", "dp"), "col"),
        ),
        check_vma=False,
    )
```
